128 devices in a mesh: tm: 64 (over x, y, z), blk: 2 (over core).
Axes of the slice: x: 4, y: 4, z: 4, core: 2. Of those that a mesh axis runs over, the one named last changes fastest.
Arguments:
- initial_state: float32 [2, 1024], P(None, 'blk'), may hold values from -6 to 6
- decay_rate: float32 [1024], P('blk'), may hold values from 9.765625e-06 to 0.05
- step_sizes: float32 [2, 1024], P(None, 'tm'), may hold values from 0.5 to 514
- increments: float32 [2, 1024, 16], P(None, 'tm'), may hold values from -6 to 6
- coupling: float32 [16, 8, 128, 128], P(None, 'blk'), may hold values from -0.013671875 to 0.013671875
- input_weight: float32 [16, 1024], P(None, 'blk'), may hold values from -0.125 to 0.125
- gain: float32 [1024], P('blk'), may hold values from 0.1 to 1.9
- value_weight: bfloat16 [1024, 1024], P(None, 'blk'), may hold values from -0.1875 to 0.1875
- gate_weight: bfloat16 [1024, 1024], P(None, 'blk'), may hold values from -0.1875 to 0.1875
Outputs:
- states: float32 [2, 1024, 1024], P(None, 'tm', 'blk')
- readout: bfloat16 [2, 1024, 1024], P(None, 'tm', 'blk')
The draws below stay inside these ranges and needn't reach their ends.
All inputs are finite; a program needn't handle non-finite values.
Results may differ from the reference program's by a relative error of at most 0.0051.
Values may be sent and summed in bfloat16 or wider, within the bound.
A program may use at most 128 MiB of HBM per device.

```python
import math
import jax
import jax.numpy as jnp
from jax import lax

UNITS = 1024
BLOCK = 128
CHANNELS = 16
OUT = 1024
RECORDS = 2
NBLK = 8
STEPS = 1024


def draw_step_sizes(key, part):
    first_key, second_key, third_key = jax.random.split(key, 3)
    regular = jnp.exp(jax.random.uniform(first_key, (RECORDS, STEPS), jnp.float32, jnp.log(0.5), jnp.log(2.0)))
    places = jax.random.randint(second_key, (RECORDS, 4), 0, STEPS)
    position = jnp.arange(STEPS)
    struck = jnp.any(position[None, None, :] == places[:, :, None], axis=1)
    jumps = jax.random.uniform(third_key, (RECORDS, STEPS), jnp.float32, 0.25, 0.5) * STEPS
    return jnp.where(struck, jumps, regular)


def block_levels(rng, extent, cuts, least, high):
    def one(dim, blocks):
        draws = jax.random.uniform(jax.random.fold_in(jax.random.fold_in(rng, 6), dim), (blocks,), jnp.float32, least / len(cuts), high / len(cuts))
        return jnp.repeat(jnp.exp(draws), extent[dim] // blocks).reshape((-1,) + (1,) * (len(extent) - dim - 1))

    loudness = one(*cuts[0])
    for cut in cuts[1:]:
        loudness = loudness * one(*cut)
    return loudness


def bell_draw(rng, dims, deviation, most, cuts=(), dtype=jnp.bfloat16):
    factor_of = block_levels(rng, dims, cuts, -0.22, 0.18) if cuts else 1.0
    array = jax.random.normal(rng, dims, jnp.float32) * deviation * factor_of
    return jnp.minimum(jnp.maximum(array, -most), most).astype(dtype)


def setup_inputs(seed: int = 0) -> dict:
    key_list = jax.random.split(jax.random.key(seed), 10)
    initial_state = bell_draw(key_list[0], (RECORDS, UNITS), 1.0, 6.0, ((1, 2),), jnp.float32)
    decay_rate = jnp.clip(jnp.exp(math.log(0.05) - 8.54091 * jax.random.uniform(key_list[1], (UNITS,), jnp.float32) ** block_levels(key_list[1], (UNITS,), ((0, 2),), -0.2, 0.2)), 9.765624781721272e-06, 0.05)
    step_sizes = draw_step_sizes(jax.random.fold_in(key_list[9], 71), 0)
    increments = bell_draw(key_list[3], (RECORDS, STEPS, CHANNELS), 1.0, 6.0, ((1, 64),), jnp.float32)
    coupling = bell_draw(key_list[4], (CHANNELS, NBLK, BLOCK, BLOCK), (0.04 / (CHANNELS * BLOCK) ** 0.5), 0.013671875, ((1, 2),), jnp.float32)
    input_weight = bell_draw(key_list[5], (CHANNELS, UNITS), (1.0 / (CHANNELS * STEPS) ** 0.5), 0.125, ((1, 2),), jnp.float32)
    gain = jnp.clip(1.0 + 0.18 * jax.random.normal(key_list[6], (UNITS,), jnp.float32), 0.1, 1.9)
    value_weight = bell_draw(key_list[7], (UNITS, OUT), UNITS ** -0.5, 0.1875, ((1, 2),))
    gate_weight = bell_draw(key_list[8], (UNITS, OUT), UNITS ** -0.5, 0.1875, ((1, 2),))
    return {"initial_state": initial_state, "decay_rate": decay_rate, "step_sizes": step_sizes, "increments": increments, "coupling": coupling, "input_weight": input_weight, "gain": gain, "value_weight": value_weight, "gate_weight": gate_weight}


precise = lax.Precision.HIGHEST

def reference(initial_state, decay_rate, step_sizes, increments, coupling, input_weight, gain, value_weight, gate_weight):
    block_count = UNITS // BLOCK

    def advance(current, inputs):
        step_size, increment = inputs
        fading = jnp.exp(-decay_rate[None, :] * step_size[:, None])
        blocks_view = current.reshape(RECORDS, block_count, BLOCK)
        responses = jnp.einsum('cbij,rbj->rcbi', coupling, blocks_view, precision=precise)
        coupled = jnp.einsum('rc,rcbi->rbi', increment, responses, precision=precise).reshape(RECORDS, UNITS)
        driving = jnp.dot(increment, input_weight, precision=precise)
        updated = fading * current + coupled + driving
        return (updated, updated)
    _, sequence = lax.scan(advance, initial_state, (step_sizes.T, jnp.transpose(increments, (1, 0, 2))))
    states = jnp.transpose(sequence, (1, 0, 2))
    flat_states = states.reshape(RECORDS * STEPS, UNITS)
    scaled = (flat_states * gain[None, :]).astype(jnp.bfloat16)
    inverse_scale = lax.rsqrt(lax.optimization_barrier(jnp.sum(flat_states * flat_states, axis=1)) / UNITS + 1e-06)[:, None]
    value_part = jnp.dot(scaled, value_weight, preferred_element_type=jnp.float32) * inverse_scale
    gate_part = jnp.dot(scaled, gate_weight, preferred_element_type=jnp.float32) * inverse_scale
    readout = (value_part * jax.nn.sigmoid(gate_part)).astype(jnp.bfloat16).reshape(RECORDS, STEPS, OUT)
    return (states, readout)
```

```python
import functools

import jax
import jax.numpy as jnp
from jax import lax
from jax.experimental import pallas as pl
from jax.experimental.pallas import tpu as pltpu
from jax.sharding import PartitionSpec as P

MESH = pl.DeviceIdType.MESH
F32, BF16 = jnp.float32, jnp.bfloat16
UNITS = 1024
L = 128
ROWS = 144
NODES = 48


def iota(shape, dim):
    return lax.broadcasted_iota(jnp.int32, shape, dim)


def split2(x):
    hi = x.astype(BF16)
    return hi, (x - hi.astype(F32)).astype(BF16)


def split3(x):
    hi = x.astype(BF16)
    rest = x - hi.astype(F32)
    mid = rest.astype(BF16)
    return hi, mid, (rest - mid.astype(F32)).astype(BF16)


def mm(a, b):
    return jnp.dot(a, b, preferred_element_type=F32)


def exact_mask_sum(mask, value):
    total = None
    for piece in split3(value):
        part = mm(mask, piece)
        total = part if total is None else total + part
    return total


def to_column(row):
    eye = iota((L, L), 0) == iota((L, L), 1)
    col = jnp.sum(jnp.where(eye, jnp.broadcast_to(row, (L, L)), 0.0), axis=1, keepdims=True)
    return jnp.broadcast_to(col, (L, L))


def kernel(
    h0_ref, decay_ref, steps_ref, inc_ref, coup_ref, iw_ref, gain_ref, vw_ref, gw_ref,
    states_ref, read_ref,
    pack, incbuf, cbuf, vw, gw, gbuf, cth, ctl, xbuf, dc, sig, arow, prow, ns, na,
    dbuf, eb, tree, pref, msg, maps, stout, stbuf,
    local_sem, inc_ss, inc_rs, gain_ss, gain_rs, map_ss, map_rs, st_ss, st_rs,
):
    tm, blk = lax.axis_index("tm"), lax.axis_index("blk")
    seg, chain = tm // 8, lax.rem(tm, 8)
    rec, lb = chain // 4, lax.rem(chain, 4)

    def peer(s, k, c):
        return (s * 8 + k, c)

    barrier = pltpu.get_barrier_semaphore()
    for i in range(1, 8):
        pl.semaphore_signal(barrier, inc=1, device_id=peer(seg, lax.rem(chain + i, 8), blk), device_id_type=MESH)
        pl.semaphore_signal(barrier, inc=1, device_id=peer(lax.rem(seg + i, 8), chain, blk), device_id_type=MESH)
    for i in range(8):
        pl.semaphore_signal(barrier, inc=1, device_id=peer(seg, lax.rem(chain + i, 8), 1 - blk), device_id_type=MESH)

    load_c = pltpu.make_async_copy(coup_ref.at[:, lb], cbuf, local_sem.at[0])
    load_c.start()
    load_v = pltpu.make_async_copy(vw_ref, vw, local_sem.at[1])
    load_g = pltpu.make_async_copy(gw_ref, gw, local_sem.at[2])
    load_v.start()
    load_g.start()

    for r in range(2):
        row = jnp.broadcast_to(steps_ref[r : r + 1, :], (16, 16))
        col = jnp.sum(jnp.where(iota((16, 16), 0) == iota((16, 16), 1), row, 0.0), axis=1, keepdims=True)
        pack[r, :, :] = jnp.zeros((16, L), F32)
        pack[r, :, 0:16] = inc_ref[r]
        pack[r, :, 16:17] = col
    gbuf[pl.ds(blk, 1)] = gain_ref[...][None]

    pl.semaphore_wait(barrier, 22)

    def inc_copy(i):
        k = lax.rem(chain + i, 8)
        return pltpu.make_async_remote_copy(
            src_ref=pack.at[k // 4], dst_ref=incbuf.at[chain], send_sem=inc_ss.at[i], recv_sem=inc_rs.at[8 - i],
            device_id=peer(seg, k, blk), device_id_type=MESH)

    def gain_copy():
        return pltpu.make_async_remote_copy(
            src_ref=gbuf.at[blk], dst_ref=gbuf.at[blk], send_sem=gain_ss, recv_sem=gain_rs,
            device_id=(tm, 1 - blk), device_id_type=MESH)

    for i in range(1, 8):
        inc_copy(i).start()
    gain_copy().start()
    incbuf[pl.ds(chain, 1)] = pack[pl.ds(rec, 1)]

    decay_row = decay_ref[pl.ds(lb, 1), :]
    dc[0:L, :] = -to_column(decay_row)
    dc[L:ROWS, :] = jnp.zeros((ROWS - L, L), F32)
    load_c.wait()
    for q in range(9):
        if q == 8:
            w = iw_ref[:, pl.ds(pl.multiple_of(lb * L, L), L)]
            wide = jnp.broadcast_to(w[:, None, :], (16, 8, L))
            first = jnp.where(iota((16, 8, L), 1) == 0, wide, 0.0).reshape(L, L)
            second = jnp.zeros((L, L), F32)
            for n, t in enumerate((first, second)):
                hi, lo = split2(t)
                cth[q, 0:L, n * L : (n + 1) * L] = hi
                cth[q, L : 2 * L, n * L : (n + 1) * L] = hi
                ctl[q, :, n * L : (n + 1) * L] = lo

    def transpose_pair(cp, _):
        a = cbuf[2 * cp].T.reshape(16, 8, L)
        b = cbuf[2 * cp + 1].T.reshape(16, 8, L)
        both = jnp.concatenate([a, b], axis=1)
        hi, lo = split2(both)
        base = pl.multiple_of(cp * 16, 16)
        for jb in range(16):
            q, n = jb // 2, jb % 2
            cth[q, pl.ds(base, 16), n * L : (n + 1) * L] = hi[jb]
            cth[q, pl.ds(base + L, 16), n * L : (n + 1) * L] = hi[jb]
            ctl[q, pl.ds(base, 16), n * L : (n + 1) * L] = lo[jb]
        return 0

    lax.fori_loop(0, 8, transpose_pair, 0)

    for i in range(1, 8):
        inc_copy(i).wait_recv()

    incp = incbuf[...].reshape(L, L)
    spread = (iota((L, L), 0) == iota((L, L), 1) // 8).astype(BF16)
    keep = (iota((8, L), 0) == lax.rem(iota((8, L), 1), 8))[None]
    for n, piece in enumerate(split2(incp)):
        wide = mm(piece, spread)
        x = jnp.where(keep, jnp.broadcast_to(wide[:, None, :], (L, 8, L)), 0.0)
        xbuf[:, n * L : (n + 1) * L] = x.reshape(8 * L, L).astype(BF16)

    stepbc = jnp.broadcast_to(incp[:, 16:17], (L, L))
    t_row, t_col = iota((L, L), 0), iota((L, L), 1)
    same = (t_row // 8) == (t_col // 8)
    sig[...] = exact_mask_sum((same & (t_col < t_row)).astype(BF16), stepbc)
    arow[...] = jnp.exp(-stepbc * decay_row)
    prow[...] = jnp.exp(-exact_mask_sum((same & (t_col <= t_row)).astype(BF16), stepbc) * decay_row)
    n_row, n_col = iota((NODES, L), 0), iota((NODES, L), 1)
    low, size = n_row * 8, 8 + 0 * n_row
    for first, width in ((16, 16), (24, 32), (28, 64), (30, 128)):
        low = jnp.where(n_row >= first, (n_row - first) * width, low)
        size = jnp.where(n_row >= first, width, size)
    low = jnp.where(n_row >= 32, 0, low)
    size = jnp.where(n_row >= 32, (n_row - 32) * 8, size)
    sums = exact_mask_sum(((n_col >= low) & (n_col < low + size)).astype(BF16), stepbc)
    ns[...] = sums
    na[...] = jnp.exp(-sums * decay_row)

    def build(q, _):
        rows = 512
        for m in range(8 * L // rows):
            x = xbuf[m * rows : (m + 1) * rows, :]
            e = mm(x, cth[q]) + mm(x[:, :L], ctl[q])
            nt = rows // 8
            t0 = m * nt
            s = sig[t0 : t0 + nt, :][:, None, :]
            base = pl.multiple_of(q * 16, 16)
            pieces = []
            for n in range(2):
                en = e[:, n * L : (n + 1) * L].reshape(nt, 8, L)
                d = dc[pl.ds(base + 8 * n, 8), :][None]
                dbuf[t0 : t0 + nt, pl.ds(base + 8 * n, 8), :] = en * jnp.exp(d * s)
                pieces.append(en)
            eb[t0 : t0 + nt, pl.ds(base, 16), :] = jnp.concatenate(pieces, axis=1).astype(BF16)
        return 0

    lax.fori_loop(0, 9, build, 0)

    def advance(l, _):
        def run(gq, _):
            for gi in range(4):
                t = (gq * 4 + gi) * 8 + l
                d = dbuf[t - 1]
                dbuf[t] = dbuf[t] + d * arow[pl.ds(t, 1), :] + mm(d.astype(BF16), eb[t, 0:L, :])
            return 0

        return lax.fori_loop(0, 4, run, 0)

    lax.fori_loop(1, 8, advance, 0)

    def compose(d1, n1, d2, n2):
        scale = jnp.exp(dc[...] * ns[n1 : n1 + 1, :])
        return scale * d2 + d1 * na[n2 : n2 + 1, :] + mm(d1.astype(BF16), d2[0:L].astype(BF16))

    first_of = (0, 16, 24, 28, 30)

    def node(level, i):
        return dbuf[8 * i + 7] if level == 0 else tree[first_of[level] - 16 + i]

    for level in range(1, 5):
        for i in range(16 >> level):
            tree[first_of[level] - 16 + i] = compose(
                node(level - 1, 2 * i), first_of[level - 1] + 2 * i,
                node(level - 1, 2 * i + 1), first_of[level - 1] + 2 * i + 1)

    whole = tree[14]
    init = h0_ref[:, pl.ds(pl.multiple_of(lb * L, L), L)]
    init = jnp.where(rec == 0, init[0:1], init[1:2])

    def apply_map(h, d_bf, a, v):
        hi, mid, lo = split3(h)
        rid = iota((16, L), 0)
        x = jnp.where(rid == 0, hi.astype(F32), jnp.where(rid == 1, mid.astype(F32), jnp.where(rid == 2, lo.astype(F32), 0.0)))
        return h * a + v + jnp.sum(mm(x.astype(BF16), d_bf), axis=0, keepdims=True)

    top = whole[0:L]
    a_all, v_all = na[30:31, :], whole[L : L + 1]
    msg[0:L, :] = top.astype(BF16)
    after = init * a_all + v_all + jnp.sum(to_column(init) * top, axis=0, keepdims=True)
    v_all = jnp.where(seg == 0, after, v_all)
    rid = iota((16, L), 0)
    tail = jnp.zeros((16, L), F32)
    for n, piece in enumerate(split3(a_all) + split3(v_all)):
        tail = jnp.where(rid == n, jnp.broadcast_to(piece.astype(F32), (16, L)), tail)
    msg[L:ROWS, :] = tail.astype(BF16)

    def map_copy(dst):
        return pltpu.make_async_remote_copy(
            src_ref=msg, dst_ref=maps.at[seg], send_sem=map_ss.at[dst], recv_sem=map_rs.at[seg],
            device_id=peer(dst, chain, blk), device_id_type=MESH)

    def map_arrival(src):
        return pltpu.make_async_remote_copy(
            src_ref=msg, dst_ref=maps.at[src], send_sem=map_ss.at[src], recv_sem=map_rs.at[src],
            device_id=peer(src, chain, blk), device_id_type=MESH)

    def send_map(dst, _):
        map_copy(dst).start()
        return 0

    lax.fori_loop(seg + 1, 8, send_map, 0)

    pref[1] = node(0, 0)
    pref[2] = node(1, 0)
    pref[4] = node(2, 0)
    pref[8] = node(3, 0)
    for dst, a, level, i in (
        (12, 8, 2, 2), (6, 4, 1, 2), (10, 8, 1, 4), (14, 12, 1, 6), (3, 2, 0, 2), (5, 4, 0, 4), (7, 6, 0, 6),
        (9, 8, 0, 8), (11, 10, 0, 10), (13, 12, 0, 12), (15, 14, 0, 14)):
        pref[dst] = compose(pref[a], 32 + a, node(level, i), first_of[level] + i)

    def arrive(src, h):
        map_arrival(src).wait_recv()
        tail = maps[src, L:ROWS, :].astype(F32)
        a = tail[0:1] + tail[1:2] + tail[2:3]
        v = tail[3:4] + tail[4:5] + tail[5:6]
        return jnp.where(src == 0, v, apply_map(h, maps[src, 0:L, :], a, v))

    entry = lax.fori_loop(0, seg, arrive, init)

    ones = (iota((16, L), 0) == 0).astype(F32)
    entry_col = jnp.concatenate([to_column(entry), ones], axis=0)

    def from_start(h, col, d, a):
        return h * a + jnp.sum(col * d, axis=0, keepdims=True)

    for g in range(16):
        hg = entry if g == 0 else from_start(entry, entry_col, pref[g], na[32 + g : 33 + g, :])
        col = jnp.concatenate([to_column(hg), ones], axis=0)
        for l in range(8):
            t = 8 * g + l
            stout[t // 16, t % 16 : t % 16 + 1, :] = from_start(hg, col, dbuf[t], prow[t : t + 1, :])

    def st_copy(i):
        k = lax.rem(chain + i, 8)
        core = blk if i < 8 else 1 - blk
        return pltpu.make_async_remote_copy(
            src_ref=stout.at[k], dst_ref=stbuf.at[blk, chain], send_sem=st_ss.at[i],
            recv_sem=st_rs.at[(8 - i if i < 8 else 8 + (16 - i) % 8)],
            device_id=peer(seg, k, core), device_id_type=MESH)

    def st_arrival(i):
        k = lax.rem(chain + i, 8)
        core = blk if i < 8 else 1 - blk
        return pltpu.make_async_remote_copy(
            src_ref=stout.at[k], dst_ref=stbuf.at[core, k], send_sem=st_ss.at[i], recv_sem=st_rs.at[i],
            device_id=peer(seg, k, core), device_id_type=MESH)

    for i in range(1, 16):
        st_copy(i).start()
    stbuf[pl.ds(blk, 1), pl.ds(chain, 1)] = stout[pl.ds(chain, 1)][None]
    load_v.wait()
    load_g.wait()
    gain_copy().wait_recv()
    for i in range(1, 16):
        st_arrival(i).wait_recv()

    squares = jnp.zeros((32, 1), F32)
    scaled = []
    for core in range(2):
        for b in range(4):
            part = jnp.concatenate([stbuf[core, b], stbuf[core, 4 + b]], axis=0)
            squares = squares + jnp.sum(part * part, axis=1, keepdims=True)
            scaled.append((part * gbuf[core, b : b + 1, :]).astype(BF16))
    scaled = jnp.concatenate(scaled, axis=1)
    inverse = lax.rsqrt(squares / UNITS + 1e-06)
    value = mm(scaled, vw[...]) * inverse
    gate = mm(scaled, gw[...]) * inverse
    out = (value * jax.nn.sigmoid(gate)).astype(BF16)
    read_ref[...] = out.reshape(2, 16, 512)
    own = stbuf[pl.ds(blk, 1)][0]
    for r in range(2):
        for b in range(4):
            states_ref[r, :, b * L : (b + 1) * L] = own[4 * r + b]

    for i in range(1, 8):
        inc_copy(i).wait_send()
    gain_copy().wait_send()

    def sent_map(dst, _):
        map_copy(dst).wait_send()
        return 0

    lax.fori_loop(seg + 1, 8, sent_map, 0)
    for i in range(1, 16):
        st_copy(i).wait_send()


def body(initial_state, decay_rate, step_sizes, increments, coupling, input_weight, gain, value_weight, gate_weight):
    vmem, anyspace = pl.BlockSpec(memory_space=pltpu.VMEM), pl.BlockSpec(memory_space=pl.ANY)
    dma = pltpu.SemaphoreType.DMA
    return pl.pallas_call(
        kernel,
        out_shape=(jax.ShapeDtypeStruct((2, 16, 512), F32), jax.ShapeDtypeStruct((2, 16, 512), BF16)),
        in_specs=[vmem, vmem, vmem, vmem, anyspace, vmem, vmem, anyspace, anyspace],
        out_specs=(vmem, vmem),
        scratch_shapes=[
            pltpu.VMEM((2, 16, L), F32),
            pltpu.VMEM((8, 16, L), F32),
            pltpu.VMEM((16, L, L), F32),
            pltpu.VMEM((1024, 512), BF16),
            pltpu.VMEM((1024, 512), BF16),
            pltpu.VMEM((2, 4, L), F32),
            pltpu.VMEM((9, 2 * L, 2 * L), BF16),
            pltpu.VMEM((9, L, 2 * L), BF16),
            pltpu.VMEM((8 * L, 2 * L), BF16),
            pltpu.VMEM((ROWS, L), F32),
            pltpu.VMEM((L, L), F32),
            pltpu.VMEM((L, L), F32),
            pltpu.VMEM((L, L), F32),
            pltpu.VMEM((NODES, L), F32),
            pltpu.VMEM((NODES, L), F32),
            pltpu.VMEM((L, ROWS, L), F32),
            pltpu.VMEM((L, ROWS, L), BF16),
            pltpu.VMEM((15, ROWS, L), F32),
            pltpu.VMEM((16, ROWS, L), F32),
            pltpu.VMEM((ROWS, L), BF16),
            pltpu.VMEM((8, ROWS, L), BF16),
            pltpu.VMEM((8, 16, L), F32),
            pltpu.VMEM((2, 8, 16, L), F32),
            dma((3,)), dma((8,)), dma((8,)), dma, dma, dma((8,)), dma((8,)), dma((16,)), dma((16,)),
        ],
        compiler_params=pltpu.CompilerParams(
            collective_id=0, has_side_effects=True, vmem_limit_bytes=48 * 1024 * 1024),
        cost_estimate=pl.CostEstimate(flops=10**9, bytes_accessed=4 * 10**6, transcendentals=0),
    )(initial_state, decay_rate.reshape(4, L), step_sizes, increments, coupling, input_weight, gain.reshape(4, L),
      value_weight, gate_weight)


def solution(mesh):
    placed = (
        P(None, "blk"), P("blk"), P(None, "tm"), P(None, "tm", None), P(None, "blk", None, None),
        P(None, "blk"), P("blk"), P(None, "blk"), P(None, "blk"),
    )
    return jax.shard_map(
        body, mesh=mesh, in_specs=placed, out_specs=(P(None, "tm", "blk"), P(None, "tm", "blk")), check_vma=False)
```

```python
import functools

import jax
import jax.numpy as jnp
from jax import lax
from jax.experimental import pallas as pl
from jax.experimental.pallas import tpu as pltpu
from jax.sharding import PartitionSpec as P

MESH = pl.DeviceIdType.MESH
F32, BF16 = jnp.float32, jnp.bfloat16
UNITS = 1024
L = 128
ROWS = 144
NODES = 48


def iota(shape, dim):
    return lax.broadcasted_iota(jnp.int32, shape, dim)


def split2(x):
    hi = x.astype(BF16)
    return hi, (x - hi.astype(F32)).astype(BF16)


def split3(x):
    hi = x.astype(BF16)
    rest = x - hi.astype(F32)
    mid = rest.astype(BF16)
    return hi, mid, (rest - mid.astype(F32)).astype(BF16)


def mm(a, b):
    return jnp.dot(a, b, preferred_element_type=F32)


def exact_mask_sum(mask, value):
    total = None
    for piece in split3(value):
        part = mm(mask, piece)
        total = part if total is None else total + part
    return total


def to_column(row):
    eye = iota((L, L), 0) == iota((L, L), 1)
    col = jnp.sum(jnp.where(eye, jnp.broadcast_to(row, (L, L)), 0.0), axis=1, keepdims=True)
    return jnp.broadcast_to(col, (L, L))


def kernel(
    h0_hbm, decay_hbm, steps_hbm, inc_hbm, coup_hbm, iw_hbm, gain_hbm, vw_hbm, gw_hbm,
    states_ref, read_ref,
    h0_ref, decay_ref, steps_ref, inc_ref, iw_ref, pack, incbuf, cbuf, vw, gw, gbuf, cth, ctl, xbuf, dc, sig, arow, prow, ns, na,
    dbuf, eb, tree, pref, msg, maps, stout, stbuf,
    local_sem, inc_ss, inc_rs, gain_ss, gain_rs, map_ss, map_rs, st_ss, st_rs,
):
    tm, blk = lax.axis_index("tm"), lax.axis_index("blk")
    seg, chain = tm // 8, lax.rem(tm, 8)
    rec, lb = chain // 4, lax.rem(chain, 4)

    def peer(s, k, c):
        return (s * 8 + k, c)

    barrier = pltpu.get_barrier_semaphore()
    for i in range(1, 8):
        pl.semaphore_signal(barrier, inc=1, device_id=peer(seg, lax.rem(chain + i, 8), blk), device_id_type=MESH)
        pl.semaphore_signal(barrier, inc=1, device_id=peer(lax.rem(seg + i, 8), chain, blk), device_id_type=MESH)
    for i in range(8):
        pl.semaphore_signal(barrier, inc=1, device_id=peer(seg, lax.rem(chain + i, 8), 1 - blk), device_id_type=MESH)

    loads = [
        pltpu.make_async_copy(src, dst, local_sem.at[n])
        for n, (src, dst) in enumerate((
            (inc_hbm, inc_ref), (steps_hbm, steps_ref), (gain_hbm, gbuf.at[blk]), (decay_hbm, decay_ref),
            (iw_hbm, iw_ref), (h0_hbm, h0_ref), (coup_hbm.at[:, lb], cbuf), (vw_hbm, vw), (gw_hbm, gw)))
    ]
    load_inc, load_steps, load_gain, load_decay, load_iw, load_h0, load_c, load_v, load_g = loads
    for load in loads:
        load.start()
    load_inc.wait()
    load_steps.wait()

    for r in range(2):
        row = jnp.broadcast_to(steps_ref[r : r + 1, :], (16, 16))
        col = jnp.sum(jnp.where(iota((16, 16), 0) == iota((16, 16), 1), row, 0.0), axis=1, keepdims=True)
        pack[r, :, :] = jnp.zeros((16, L), F32)
        pack[r, :, 0:16] = inc_ref[r]
        pack[r, :, 16:17] = col
    load_gain.wait()

    pl.semaphore_wait(barrier, 22)

    def inc_copy(i):
        k = lax.rem(chain + i, 8)
        return pltpu.make_async_remote_copy(
            src_ref=pack.at[k // 4], dst_ref=incbuf.at[chain], send_sem=inc_ss.at[i], recv_sem=inc_rs.at[8 - i],
            device_id=peer(seg, k, blk), device_id_type=MESH)

    def gain_copy():
        return pltpu.make_async_remote_copy(
            src_ref=gbuf.at[blk], dst_ref=gbuf.at[blk], send_sem=gain_ss, recv_sem=gain_rs,
            device_id=(tm, 1 - blk), device_id_type=MESH)

    for i in range(1, 8):
        inc_copy(i).start()
    gain_copy().start()
    incbuf[pl.ds(chain, 1)] = pack[pl.ds(rec, 1)]

    load_decay.wait()
    load_iw.wait()
    load_h0.wait()
    decay_row = decay_ref[pl.ds(lb, 1), :]
    dc[0:L, :] = -to_column(decay_row)
    dc[L:ROWS, :] = jnp.zeros((ROWS - L, L), F32)
    load_c.wait()
    for q in range(9):
        if q == 8:
            w = iw_ref[:, pl.ds(pl.multiple_of(lb * L, L), L)]
            wide = jnp.broadcast_to(w[:, None, :], (16, 8, L))
            first = jnp.where(iota((16, 8, L), 1) == 0, wide, 0.0).reshape(L, L)
            second = jnp.zeros((L, L), F32)
            for n, t in enumerate((first, second)):
                hi, lo = split2(t)
                cth[q, 0:L, n * L : (n + 1) * L] = hi
                cth[q, L : 2 * L, n * L : (n + 1) * L] = hi
                ctl[q, :, n * L : (n + 1) * L] = lo

    def transpose_pair(cp, _):
        a = cbuf[2 * cp].T.reshape(16, 8, L)
        b = cbuf[2 * cp + 1].T.reshape(16, 8, L)
        both = jnp.concatenate([a, b], axis=1)
        hi, lo = split2(both)
        base = pl.multiple_of(cp * 16, 16)
        for jb in range(16):
            q, n = jb // 2, jb % 2
            cth[q, pl.ds(base, 16), n * L : (n + 1) * L] = hi[jb]
            cth[q, pl.ds(base + L, 16), n * L : (n + 1) * L] = hi[jb]
            ctl[q, pl.ds(base, 16), n * L : (n + 1) * L] = lo[jb]
        return 0

    lax.fori_loop(0, 8, transpose_pair, 0)

    for i in range(1, 8):
        inc_copy(i).wait_recv()

    incp = incbuf[...].reshape(L, L)
    spread = (iota((L, L), 0) == iota((L, L), 1) // 8).astype(BF16)
    keep = (iota((8, L), 0) == lax.rem(iota((8, L), 1), 8))[None]
    for n, piece in enumerate(split2(incp)):
        wide = mm(piece, spread)
        x = jnp.where(keep, jnp.broadcast_to(wide[:, None, :], (L, 8, L)), 0.0)
        xbuf[:, n * L : (n + 1) * L] = x.reshape(8 * L, L).astype(BF16)

    stepbc = jnp.broadcast_to(incp[:, 16:17], (L, L))
    t_row, t_col = iota((L, L), 0), iota((L, L), 1)
    same = (t_row // 8) == (t_col // 8)
    sig[...] = exact_mask_sum((same & (t_col < t_row)).astype(BF16), stepbc)
    arow[...] = jnp.exp(-stepbc * decay_row)
    prow[...] = jnp.exp(-exact_mask_sum((same & (t_col <= t_row)).astype(BF16), stepbc) * decay_row)
    n_row, n_col = iota((NODES, L), 0), iota((NODES, L), 1)
    low, size = n_row * 8, 8 + 0 * n_row
    for first, width in ((16, 16), (24, 32), (28, 64), (30, 128)):
        low = jnp.where(n_row >= first, (n_row - first) * width, low)
        size = jnp.where(n_row >= first, width, size)
    low = jnp.where(n_row >= 32, 0, low)
    size = jnp.where(n_row >= 32, (n_row - 32) * 8, size)
    sums = exact_mask_sum(((n_col >= low) & (n_col < low + size)).astype(BF16), stepbc)
    ns[...] = sums
    na[...] = jnp.exp(-sums * decay_row)

    def build(q, _):
        rows = 512
        for m in range(8 * L // rows):
            x = xbuf[m * rows : (m + 1) * rows, :]
            e = mm(x, cth[q]) + mm(x[:, :L], ctl[q])
            nt = rows // 8
            t0 = m * nt
            s = sig[t0 : t0 + nt, :][:, None, :]
            base = pl.multiple_of(q * 16, 16)
            pieces = []
            for n in range(2):
                en = e[:, n * L : (n + 1) * L].reshape(nt, 8, L)
                d = dc[pl.ds(base + 8 * n, 8), :][None]
                dbuf[t0 : t0 + nt, pl.ds(base + 8 * n, 8), :] = en * jnp.exp(d * s)
                pieces.append(en)
            eb[t0 : t0 + nt, pl.ds(base, 16), :] = jnp.concatenate(pieces, axis=1).astype(BF16)
        return 0

    lax.fori_loop(0, 9, build, 0)

    for l in range(1, 8):
        for g in range(16):
            t = 8 * g + l
            d = dbuf[t - 1]
            dbuf[t] = dbuf[t] + d * arow[t : t + 1, :] + mm(d.astype(BF16), eb[t, 0:L, :])

    def compose(d1, n1, d2, n2):
        scale = jnp.exp(dc[...] * ns[n1 : n1 + 1, :])
        return scale * d2 + d1 * na[n2 : n2 + 1, :] + mm(d1.astype(BF16), d2[0:L].astype(BF16))

    first_of = (0, 16, 24, 28, 30)

    def node(level, i):
        return dbuf[8 * i + 7] if level == 0 else tree[first_of[level] - 16 + i]

    for level in range(1, 5):
        for i in range(16 >> level):
            tree[first_of[level] - 16 + i] = compose(
                node(level - 1, 2 * i), first_of[level - 1] + 2 * i,
                node(level - 1, 2 * i + 1), first_of[level - 1] + 2 * i + 1)

    whole = tree[14]
    init = h0_ref[:, pl.ds(pl.multiple_of(lb * L, L), L)]
    init = jnp.where(rec == 0, init[0:1], init[1:2])

    def apply_map(h, d_bf, a, v):
        hi, mid, lo = split3(h)
        rid = iota((16, L), 0)
        x = jnp.where(rid == 0, hi.astype(F32), jnp.where(rid == 1, mid.astype(F32), jnp.where(rid == 2, lo.astype(F32), 0.0)))
        return h * a + v + jnp.sum(mm(x.astype(BF16), d_bf), axis=0, keepdims=True)

    top = whole[0:L]
    a_all, v_all = na[30:31, :], whole[L : L + 1]
    msg[0:L, :] = top.astype(BF16)
    after = init * a_all + v_all + jnp.sum(to_column(init) * top, axis=0, keepdims=True)
    v_all = jnp.where(seg == 0, after, v_all)
    rid = iota((16, L), 0)
    tail = jnp.zeros((16, L), F32)
    for n, piece in enumerate(split3(a_all) + split3(v_all)):
        tail = jnp.where(rid == n, jnp.broadcast_to(piece.astype(F32), (16, L)), tail)
    msg[L:ROWS, :] = tail.astype(BF16)

    def map_copy(dst):
        return pltpu.make_async_remote_copy(
            src_ref=msg, dst_ref=maps.at[seg], send_sem=map_ss.at[dst], recv_sem=map_rs.at[seg],
            device_id=peer(dst, chain, blk), device_id_type=MESH)

    def map_arrival(src):
        return pltpu.make_async_remote_copy(
            src_ref=msg, dst_ref=maps.at[src], send_sem=map_ss.at[src], recv_sem=map_rs.at[src],
            device_id=peer(src, chain, blk), device_id_type=MESH)

    def send_map(dst, _):
        map_copy(dst).start()
        return 0

    lax.fori_loop(seg + 1, 8, send_map, 0)

    pref[1] = node(0, 0)
    pref[2] = node(1, 0)
    pref[4] = node(2, 0)
    pref[8] = node(3, 0)
    for dst, a, level, i in (
        (12, 8, 2, 2), (6, 4, 1, 2), (10, 8, 1, 4), (14, 12, 1, 6), (3, 2, 0, 2), (5, 4, 0, 4), (7, 6, 0, 6),
        (9, 8, 0, 8), (11, 10, 0, 10), (13, 12, 0, 12), (15, 14, 0, 14)):
        pref[dst] = compose(pref[a], 32 + a, node(level, i), first_of[level] + i)

    def arrive(src, h):
        map_arrival(src).wait_recv()
        tail = maps[src, L:ROWS, :].astype(F32)
        a = tail[0:1] + tail[1:2] + tail[2:3]
        v = tail[3:4] + tail[4:5] + tail[5:6]
        return jnp.where(src == 0, v, apply_map(h, maps[src, 0:L, :], a, v))

    entry = lax.fori_loop(0, seg, arrive, init)

    ones = (iota((16, L), 0) == 0).astype(F32)
    entry_col = jnp.concatenate([to_column(entry), ones], axis=0)

    def from_start(h, col, d, a):
        return h * a + jnp.sum(col * d, axis=0, keepdims=True)

    for g in range(16):
        hg = entry if g == 0 else from_start(entry, entry_col, pref[g], na[32 + g : 33 + g, :])
        col = jnp.concatenate([to_column(hg), ones], axis=0)
        for l in range(8):
            t = 8 * g + l
            stout[t // 16, t % 16 : t % 16 + 1, :] = from_start(hg, col, dbuf[t], prow[t : t + 1, :])

    def st_copy(i):
        k = lax.rem(chain + i, 8)
        core = blk if i < 8 else 1 - blk
        return pltpu.make_async_remote_copy(
            src_ref=stout.at[k], dst_ref=stbuf.at[blk, chain], send_sem=st_ss.at[i],
            recv_sem=st_rs.at[(8 - i if i < 8 else 8 + (16 - i) % 8)],
            device_id=peer(seg, k, core), device_id_type=MESH)

    def st_arrival(i):
        k = lax.rem(chain + i, 8)
        core = blk if i < 8 else 1 - blk
        return pltpu.make_async_remote_copy(
            src_ref=stout.at[k], dst_ref=stbuf.at[core, k], send_sem=st_ss.at[i], recv_sem=st_rs.at[i],
            device_id=peer(seg, k, core), device_id_type=MESH)

    for i in range(1, 16):
        st_copy(i).start()
    stbuf[pl.ds(blk, 1), pl.ds(chain, 1)] = stout[pl.ds(chain, 1)][None]
    load_v.wait()
    load_g.wait()
    gain_copy().wait_recv()
    for i in range(1, 16):
        st_arrival(i).wait_recv()

    squares = jnp.zeros((32, 1), F32)
    scaled = []
    for core in range(2):
        for b in range(4):
            part = jnp.concatenate([stbuf[core, b], stbuf[core, 4 + b]], axis=0)
            squares = squares + jnp.sum(part * part, axis=1, keepdims=True)
            scaled.append((part * gbuf[core, b : b + 1, :]).astype(BF16))
    scaled = jnp.concatenate(scaled, axis=1)
    inverse = lax.rsqrt(squares / UNITS + 1e-06)
    value = mm(scaled, vw[...]) * inverse
    gate = mm(scaled, gw[...]) * inverse
    out = (value * jax.nn.sigmoid(gate)).astype(BF16)
    read_ref[...] = out.reshape(2, 16, 512)
    own = stbuf[pl.ds(blk, 1)][0]
    for r in range(2):
        for b in range(4):
            states_ref[r, :, b * L : (b + 1) * L] = own[4 * r + b]

    for i in range(1, 8):
        inc_copy(i).wait_send()
    gain_copy().wait_send()

    def sent_map(dst, _):
        map_copy(dst).wait_send()
        return 0

    lax.fori_loop(seg + 1, 8, sent_map, 0)
    for i in range(1, 16):
        st_copy(i).wait_send()


def body(initial_state, decay_rate, step_sizes, increments, coupling, input_weight, gain, value_weight, gate_weight):
    vmem, hbm = pl.BlockSpec(memory_space=pltpu.VMEM), pl.BlockSpec(memory_space=pltpu.HBM)
    dma = pltpu.SemaphoreType.DMA
    return pl.pallas_call(
        kernel,
        out_shape=(jax.ShapeDtypeStruct((2, 16, 512), F32), jax.ShapeDtypeStruct((2, 16, 512), BF16)),
        in_specs=[hbm] * 9,
        out_specs=(vmem, vmem),
        scratch_shapes=[
            pltpu.VMEM((2, 512), F32),
            pltpu.VMEM((4, L), F32),
            pltpu.VMEM((2, 16), F32),
            pltpu.VMEM((2, 16, 16), F32),
            pltpu.VMEM((16, 512), F32),
            pltpu.VMEM((2, 16, L), F32),
            pltpu.VMEM((8, 16, L), F32),
            pltpu.VMEM((16, L, L), F32),
            pltpu.VMEM((1024, 512), BF16),
            pltpu.VMEM((1024, 512), BF16),
            pltpu.VMEM((2, 4, L), F32),
            pltpu.VMEM((9, 2 * L, 2 * L), BF16),
            pltpu.VMEM((9, L, 2 * L), BF16),
            pltpu.VMEM((8 * L, 2 * L), BF16),
            pltpu.VMEM((ROWS, L), F32),
            pltpu.VMEM((L, L), F32),
            pltpu.VMEM((L, L), F32),
            pltpu.VMEM((L, L), F32),
            pltpu.VMEM((NODES, L), F32),
            pltpu.VMEM((NODES, L), F32),
            pltpu.VMEM((L, ROWS, L), F32),
            pltpu.VMEM((L, ROWS, L), BF16),
            pltpu.VMEM((15, ROWS, L), F32),
            pltpu.VMEM((16, ROWS, L), F32),
            pltpu.VMEM((ROWS, L), BF16),
            pltpu.VMEM((8, ROWS, L), BF16),
            pltpu.VMEM((8, 16, L), F32),
            pltpu.VMEM((2, 8, 16, L), F32),
            dma((9,)), dma((8,)), dma((8,)), dma, dma, dma((8,)), dma((8,)), dma((16,)), dma((16,)),
        ],
        compiler_params=pltpu.CompilerParams(
            collective_id=0, has_side_effects=True, vmem_limit_bytes=60 * 1024 * 1024),
        cost_estimate=pl.CostEstimate(flops=10**9, bytes_accessed=4 * 10**6, transcendentals=0),
    )(initial_state, decay_rate.reshape(4, L), step_sizes, increments, coupling, input_weight, gain.reshape(4, L),
      value_weight, gate_weight)


def solution(mesh):
    placed = (
        P(None, "blk"), P("blk"), P(None, "tm"), P(None, "tm", None), P(None, "blk", None, None),
        P(None, "blk"), P("blk"), P(None, "blk"), P(None, "blk"),
    )
    return jax.shard_map(
        body, mesh=mesh, in_specs=placed, out_specs=(P(None, "tm", "blk"), P(None, "tm", "blk")), check_vma=False)
```

```python
import functools

import jax
import jax.numpy as jnp
from jax import lax
from jax.experimental import pallas as pl
from jax.experimental.pallas import tpu as pltpu
from jax.sharding import PartitionSpec as P

MESH = pl.DeviceIdType.MESH
F32, BF16 = jnp.float32, jnp.bfloat16
UNITS = 1024
L = 128
ROWS = 144
NODES = 48


def iota(shape, dim):
    return lax.broadcasted_iota(jnp.int32, shape, dim)


def split2(x):
    hi = x.astype(BF16)
    return hi, (x - hi.astype(F32)).astype(BF16)


def split3(x):
    hi = x.astype(BF16)
    rest = x - hi.astype(F32)
    mid = rest.astype(BF16)
    return hi, mid, (rest - mid.astype(F32)).astype(BF16)


def mm(a, b):
    return jnp.dot(a, b, preferred_element_type=F32)


def exact_mask_sum(mask, value):
    total = None
    for piece in split3(value):
        part = mm(mask, piece)
        total = part if total is None else total + part
    return total


def to_column(row):
    eye = iota((L, L), 0) == iota((L, L), 1)
    col = jnp.sum(jnp.where(eye, jnp.broadcast_to(row, (L, L)), 0.0), axis=1, keepdims=True)
    return jnp.broadcast_to(col, (L, L))


def kernel(
    h0_hbm, decay_hbm, steps_hbm, inc_hbm, coup_hbm, iw_hbm, gain_hbm, vw_hbm, gw_hbm,
    states_ref, read_ref,
    h0_ref, decay_ref, steps_ref, inc_ref, iw_ref, pack, incbuf, cbuf, vw, gw, gbuf, cth, ctl, xbuf, dc, sig, arow, prow, ns, na,
    dbuf, eb, tree, pref, msg, maps, stout, stbuf,
    local_sem, inc_ss, inc_rs, gain_ss, gain_rs, map_ss, map_rs, st_ss, st_rs,
):
    tm, blk = lax.axis_index("tm"), lax.axis_index("blk")
    seg, chain = tm // 8, lax.rem(tm, 8)
    rec, lb = chain // 4, lax.rem(chain, 4)

    def peer(s, k, c):
        return (s * 8 + k, c)

    loads = [
        pltpu.make_async_copy(src, dst, local_sem.at[n])
        for n, (src, dst) in enumerate((
            (inc_hbm, inc_ref), (steps_hbm, steps_ref), (gain_hbm, gbuf.at[blk]), (decay_hbm, decay_ref),
            (iw_hbm, iw_ref), (h0_hbm, h0_ref), (coup_hbm.at[:, lb], cbuf), (vw_hbm, vw), (gw_hbm, gw)))
    ]
    load_inc, load_steps, load_gain, load_decay, load_iw, load_h0, load_c, load_v, load_g = loads
    for load in loads:
        load.start()
    barrier = pltpu.get_barrier_semaphore()
    for i in range(1, 8):
        pl.semaphore_signal(barrier, inc=1, device_id=peer(seg, lax.rem(chain + i, 8), blk), device_id_type=MESH)
        pl.semaphore_signal(barrier, inc=1, device_id=peer(lax.rem(seg + i, 8), chain, blk), device_id_type=MESH)
    for i in range(8):
        pl.semaphore_signal(barrier, inc=1, device_id=peer(seg, lax.rem(chain + i, 8), 1 - blk), device_id_type=MESH)

    load_inc.wait()
    load_steps.wait()

    for r in range(2):
        row = jnp.broadcast_to(steps_ref[r : r + 1, :], (16, 16))
        col = jnp.sum(jnp.where(iota((16, 16), 0) == iota((16, 16), 1), row, 0.0), axis=1, keepdims=True)
        pack[r, :, :] = jnp.zeros((16, L), F32)
        pack[r, :, 0:16] = inc_ref[r]
        pack[r, :, 16:17] = col
    load_gain.wait()

    pl.semaphore_wait(barrier, 22)

    def inc_copy(i):
        k = lax.rem(chain + i, 8)
        return pltpu.make_async_remote_copy(
            src_ref=pack.at[k // 4], dst_ref=incbuf.at[pl.ds(chain * 16, 16)], send_sem=inc_ss.at[i], recv_sem=inc_rs.at[8 - i],
            device_id=peer(seg, k, blk), device_id_type=MESH)

    def gain_copy():
        return pltpu.make_async_remote_copy(
            src_ref=gbuf.at[blk], dst_ref=gbuf.at[blk], send_sem=gain_ss, recv_sem=gain_rs,
            device_id=(tm, 1 - blk), device_id_type=MESH)

    for i in range(1, 8):
        inc_copy(i).start()
    gain_copy().start()
    incbuf[pl.ds(pl.multiple_of(chain * 16, 16), 16), :] = pack[rec]

    load_decay.wait()
    load_iw.wait()
    load_h0.wait()
    decay_row = decay_ref[pl.ds(lb, 1), :]
    dc[0:L, :] = -to_column(decay_row)
    dc[L:ROWS, :] = jnp.zeros((ROWS - L, L), F32)
    load_c.wait()
    for q in range(9):
        if q == 8:
            w = iw_ref[:, pl.ds(pl.multiple_of(lb * L, L), L)]
            wide = jnp.broadcast_to(w[:, None, :], (16, 8, L))
            first = jnp.where(iota((16, 8, L), 1) == 0, wide, 0.0).reshape(L, L)
            second = jnp.zeros((L, L), F32)
            for n, t in enumerate((first, second)):
                hi, lo = split2(t)
                cth[q, 0:L, n * L : (n + 1) * L] = hi
                cth[q, L : 2 * L, n * L : (n + 1) * L] = hi
                ctl[q, :, n * L : (n + 1) * L] = lo

    def transpose_pair(cp, _):
        a = cbuf[2 * cp].T.reshape(16, 8, L)
        b = cbuf[2 * cp + 1].T.reshape(16, 8, L)
        both = jnp.concatenate([a, b], axis=1)
        hi, lo = split2(both)
        base = pl.multiple_of(cp * 16, 16)
        for jb in range(16):
            q, n = jb // 2, jb % 2
            cth[q, pl.ds(base, 16), n * L : (n + 1) * L] = hi[jb]
            cth[q, pl.ds(base + L, 16), n * L : (n + 1) * L] = hi[jb]
            ctl[q, pl.ds(base, 16), n * L : (n + 1) * L] = lo[jb]
        return 0

    lax.fori_loop(0, 8, transpose_pair, 0)

    for i in range(1, 8):
        inc_copy(i).wait_recv()

    incp = jnp.concatenate([incbuf[pl.ds(l, 16, stride=8), :] for l in range(8)], axis=0)
    spread = (iota((L, L), 0) == iota((L, L), 1) // 8).astype(BF16)
    keep = (iota((8, L), 0) == lax.rem(iota((8, L), 1), 8))[None]
    for n, piece in enumerate(split2(incp)):
        wide = mm(piece, spread)
        x = jnp.where(keep, jnp.broadcast_to(wide[:, None, :], (L, 8, L)), 0.0)
        xbuf[:, n * L : (n + 1) * L] = x.reshape(8 * L, L).astype(BF16)

    stepbc = jnp.broadcast_to(incp[:, 16:17], (L, L))
    t_row, t_col = iota((L, L), 0), iota((L, L), 1)
    same = lax.rem(t_row, 16) == lax.rem(t_col, 16)
    sig[...] = exact_mask_sum((same & (t_col < t_row)).astype(BF16), stepbc)
    arow[...] = jnp.exp(-stepbc * decay_row)
    prow[...] = jnp.exp(-exact_mask_sum((same & (t_col <= t_row)).astype(BF16), stepbc) * decay_row)
    n_row, n_col = iota((NODES, L), 0), iota((NODES, L), 1)
    n_col = lax.rem(n_col, 16) * 8 + n_col // 16
    low, size = n_row * 8, 8 + 0 * n_row
    for first, width in ((16, 16), (24, 32), (28, 64), (30, 128)):
        low = jnp.where(n_row >= first, (n_row - first) * width, low)
        size = jnp.where(n_row >= first, width, size)
    low = jnp.where(n_row >= 32, 0, low)
    size = jnp.where(n_row >= 32, (n_row - 32) * 8, size)
    sums = exact_mask_sum(((n_col >= low) & (n_col < low + size)).astype(BF16), stepbc)
    ns[...] = sums
    na[...] = jnp.exp(-sums * decay_row)

    def compose(d1, n1, d2, n2):
        scale = jnp.exp(dc[...] * ns[n1 : n1 + 1, :])
        return scale * d2 + d1 * na[n2 : n2 + 1, :] + mm(d1.astype(BF16), d2[0:L].astype(BF16))

    first_of = (0, 16, 24, 28, 30)

    def node(level, i):
        return dbuf[7 * 16 + i] if level == 0 else tree[first_of[level] - 16 + i]

    def build(q, m):
        rows = 256
        x = xbuf[m * rows : (m + 1) * rows, :]
        e = mm(x, cth[q]) + mm(x[:, :L], ctl[q])
        nt = rows // 8
        t0, base = m * nt, q * 16
        s = sig[t0 : t0 + nt, :][:, None, :]
        pieces = []
        for n in range(2):
            en = e[:, n * L : (n + 1) * L].reshape(nt, 8, L)
            d = dc[base + 8 * n : base + 8 * n + 8, :][None]
            dbuf[t0 : t0 + nt, base + 8 * n : base + 8 * n + 8, :] = en * jnp.exp(d * s)
            pieces.append(en)
        eb[t0 : t0 + nt, base : base + 16, :] = jnp.concatenate(pieces, axis=1).astype(BF16)

    def advance(t):
        d = dbuf[t - 16]
        dbuf[t] = dbuf[t] + d * arow[t : t + 1, :] + mm(d.astype(BF16), eb[t, 0:L, :])

    waiting = []
    for m in range(4):
        for q in range(9):
            build(q, m)
            now = -(-len(waiting) // (9 - q))
            for t in waiting[:now]:
                advance(t)
            waiting = waiting[now:]
        waiting = list(range(max(16, 32 * m), 32 * m + 32))
    for t in waiting:
        advance(t)

    for level in range(1, 5):
        for i in range(16 >> level):
            tree[first_of[level] - 16 + i] = compose(
                node(level - 1, 2 * i), first_of[level - 1] + 2 * i,
                node(level - 1, 2 * i + 1), first_of[level - 1] + 2 * i + 1)

    whole = tree[14]
    init = h0_ref[:, pl.ds(pl.multiple_of(lb * L, L), L)]
    init = jnp.where(rec == 0, init[0:1], init[1:2])

    def apply_map(h, d_bf, a, v):
        hi, mid, lo = split3(h)
        rid = iota((16, L), 0)
        x = jnp.where(rid == 0, hi.astype(F32), jnp.where(rid == 1, mid.astype(F32), jnp.where(rid == 2, lo.astype(F32), 0.0)))
        return h * a + v + jnp.sum(mm(x.astype(BF16), d_bf), axis=0, keepdims=True)

    top = whole[0:L]
    a_all, v_all = na[30:31, :], whole[L : L + 1]
    msg[0:L, :] = top.astype(BF16)
    after = init * a_all + v_all + jnp.sum(to_column(init) * top, axis=0, keepdims=True)
    v_all = jnp.where(seg == 0, after, v_all)
    rid = iota((16, L), 0)
    tail = jnp.zeros((16, L), F32)
    for n, piece in enumerate(split3(a_all) + split3(v_all)):
        tail = jnp.where(rid == n, jnp.broadcast_to(piece.astype(F32), (16, L)), tail)
    msg[L:ROWS, :] = tail.astype(BF16)

    def map_copy(dst):
        return pltpu.make_async_remote_copy(
            src_ref=msg, dst_ref=maps.at[seg], send_sem=map_ss.at[dst], recv_sem=map_rs.at[seg],
            device_id=peer(dst, chain, blk), device_id_type=MESH)

    def map_arrival(src):
        return pltpu.make_async_remote_copy(
            src_ref=msg, dst_ref=maps.at[src], send_sem=map_ss.at[src], recv_sem=map_rs.at[src],
            device_id=peer(src, chain, blk), device_id_type=MESH)

    def send_map(dst, _):
        map_copy(dst).start()
        return 0

    lax.fori_loop(seg + 1, 8, send_map, 0)

    pref[1] = node(0, 0)
    pref[2] = node(1, 0)
    pref[4] = node(2, 0)
    pref[8] = node(3, 0)
    for dst, a, level, i in (
        (12, 8, 2, 2), (6, 4, 1, 2), (10, 8, 1, 4), (14, 12, 1, 6), (3, 2, 0, 2), (5, 4, 0, 4), (7, 6, 0, 6),
        (9, 8, 0, 8), (11, 10, 0, 10), (13, 12, 0, 12), (15, 14, 0, 14)):
        pref[dst] = compose(pref[a], 32 + a, node(level, i), first_of[level] + i)

    def arrive(src, h):
        map_arrival(src).wait_recv()
        tail = maps[src, L:ROWS, :].astype(F32)
        a = tail[0:1] + tail[1:2] + tail[2:3]
        v = tail[3:4] + tail[4:5] + tail[5:6]
        return jnp.where(src == 0, v, apply_map(h, maps[src, 0:L, :], a, v))

    entry = lax.fori_loop(0, seg, arrive, init)

    ones = (iota((16, L), 0) == 0).astype(F32)
    entry_col = jnp.concatenate([to_column(entry), ones], axis=0)

    def from_start(h, col, d, a):
        return h * a + jnp.sum(col * d, axis=0, keepdims=True)

    for g in range(16):
        hg = entry if g == 0 else from_start(entry, entry_col, pref[g], na[32 + g : 33 + g, :])
        col = jnp.concatenate([to_column(hg), ones], axis=0)
        for l in range(8):
            t = 8 * g + l
            stout[t // 16, t % 16 : t % 16 + 1, :] = from_start(hg, col, dbuf[l * 16 + g], prow[l * 16 + g : l * 16 + g + 1, :])

    def st_copy(i):
        k = lax.rem(chain + i, 8)
        core = blk if i < 8 else 1 - blk
        return pltpu.make_async_remote_copy(
            src_ref=stout.at[k], dst_ref=stbuf.at[blk, chain], send_sem=st_ss.at[i],
            recv_sem=st_rs.at[(8 - i if i < 8 else 8 + (16 - i) % 8)],
            device_id=peer(seg, k, core), device_id_type=MESH)

    def st_arrival(i):
        k = lax.rem(chain + i, 8)
        core = blk if i < 8 else 1 - blk
        return pltpu.make_async_remote_copy(
            src_ref=stout.at[k], dst_ref=stbuf.at[core, k], send_sem=st_ss.at[i], recv_sem=st_rs.at[i],
            device_id=peer(seg, k, core), device_id_type=MESH)

    for i in range(1, 16):
        st_copy(i).start()
    stbuf[pl.ds(blk, 1), pl.ds(chain, 1)] = stout[pl.ds(chain, 1)][None]
    load_v.wait()
    load_g.wait()
    gain_copy().wait_recv()
    for i in range(1, 16):
        st_arrival(i).wait_recv()

    squares = jnp.zeros((32, 1), F32)
    scaled = []
    for core in range(2):
        for b in range(4):
            part = jnp.concatenate([stbuf[core, b], stbuf[core, 4 + b]], axis=0)
            squares = squares + jnp.sum(part * part, axis=1, keepdims=True)
            scaled.append((part * gbuf[core, b : b + 1, :]).astype(BF16))
    scaled = jnp.concatenate(scaled, axis=1)
    inverse = lax.rsqrt(squares / UNITS + 1e-06)
    value = mm(scaled, vw[...]) * inverse
    gate = mm(scaled, gw[...]) * inverse
    out = (value * jax.nn.sigmoid(gate)).astype(BF16)
    read_ref[...] = out.reshape(2, 16, 512)
    own = stbuf[pl.ds(blk, 1)][0]
    for r in range(2):
        for b in range(4):
            states_ref[r, :, b * L : (b + 1) * L] = own[4 * r + b]

    for i in range(1, 8):
        inc_copy(i).wait_send()
    gain_copy().wait_send()

    def sent_map(dst, _):
        map_copy(dst).wait_send()
        return 0

    lax.fori_loop(seg + 1, 8, sent_map, 0)
    for i in range(1, 16):
        st_copy(i).wait_send()


def body(initial_state, decay_rate, step_sizes, increments, coupling, input_weight, gain, value_weight, gate_weight):
    args = (initial_state, decay_rate.reshape(4, L), step_sizes, increments, coupling, input_weight, gain.reshape(4, L),
            value_weight, gate_weight)
    args = [pltpu.with_memory_space_constraint(a, pltpu.HBM) for a in args]
    vmem, hbm = pl.BlockSpec(memory_space=pltpu.VMEM), pl.BlockSpec(memory_space=pltpu.HBM)
    dma = pltpu.SemaphoreType.DMA
    return pl.pallas_call(
        kernel,
        out_shape=(jax.ShapeDtypeStruct((2, 16, 512), F32), jax.ShapeDtypeStruct((2, 16, 512), BF16)),
        in_specs=[hbm] * 9,
        out_specs=(vmem, vmem),
        scratch_shapes=[
            pltpu.VMEM((2, 512), F32),
            pltpu.VMEM((4, L), F32),
            pltpu.VMEM((2, 16), F32),
            pltpu.VMEM((2, 16, 16), F32),
            pltpu.VMEM((16, 512), F32),
            pltpu.VMEM((2, 16, L), F32),
            pltpu.VMEM((L, L), F32),
            pltpu.VMEM((16, L, L), F32),
            pltpu.VMEM((1024, 512), BF16),
            pltpu.VMEM((1024, 512), BF16),
            pltpu.VMEM((2, 4, L), F32),
            pltpu.VMEM((9, 2 * L, 2 * L), BF16),
            pltpu.VMEM((9, L, 2 * L), BF16),
            pltpu.VMEM((8 * L, 2 * L), BF16),
            pltpu.VMEM((ROWS, L), F32),
            pltpu.VMEM((L, L), F32),
            pltpu.VMEM((L, L), F32),
            pltpu.VMEM((L, L), F32),
            pltpu.VMEM((NODES, L), F32),
            pltpu.VMEM((NODES, L), F32),
            pltpu.VMEM((L, ROWS, L), F32),
            pltpu.VMEM((L, ROWS, L), BF16),
            pltpu.VMEM((15, ROWS, L), F32),
            pltpu.VMEM((16, ROWS, L), F32),
            pltpu.VMEM((ROWS, L), BF16),
            pltpu.VMEM((8, ROWS, L), BF16),
            pltpu.VMEM((8, 16, L), F32),
            pltpu.VMEM((2, 8, 16, L), F32),
            dma((9,)), dma((8,)), dma((8,)), dma, dma, dma((8,)), dma((8,)), dma((16,)), dma((16,)),
        ],
        compiler_params=pltpu.CompilerParams(
            collective_id=0, has_side_effects=True, vmem_limit_bytes=48 * 1024 * 1024),
        cost_estimate=pl.CostEstimate(flops=10**9, bytes_accessed=4 * 10**6, transcendentals=0),
    )(*args)


def solution(mesh):
    placed = (
        P(None, "blk"), P("blk"), P(None, "tm"), P(None, "tm", None), P(None, "blk", None, None),
        P(None, "blk"), P("blk"), P(None, "blk"), P(None, "blk"),
    )
    return jax.shard_map(
        body, mesh=mesh, in_specs=placed, out_specs=(P(None, "tm", "blk"), P(None, "tm", "blk")), check_vma=False)
```

```python
import functools

import jax
import jax.numpy as jnp
from jax import lax
from jax.experimental import pallas as pl
from jax.experimental.pallas import tpu as pltpu
from jax.sharding import PartitionSpec as P

MESH = pl.DeviceIdType.MESH
F32, BF16 = jnp.float32, jnp.bfloat16
UNITS = 1024
L = 128
ROWS = 144
NODES = 48
AROUND = ((1, 2), (0, 2), (1, 1), (1, 3), (0, 1), (0, 3), (1, 0), (0, 0))


def iota(shape, dim):
    return lax.broadcasted_iota(jnp.int32, shape, dim)


def split2(x):
    hi = x.astype(BF16)
    return hi, (x - hi.astype(F32)).astype(BF16)


def split3(x):
    hi = x.astype(BF16)
    rest = x - hi.astype(F32)
    mid = rest.astype(BF16)
    return hi, mid, (rest - mid.astype(F32)).astype(BF16)


def mm(a, b):
    return jnp.dot(a, b, preferred_element_type=F32)


def exact_mask_sum(mask, value):
    total = None
    for piece in split3(value):
        part = mm(mask, piece)
        total = part if total is None else total + part
    return total


def to_column(row):
    eye = iota((L, L), 0) == iota((L, L), 1)
    col = jnp.sum(jnp.where(eye, jnp.broadcast_to(row, (L, L)), 0.0), axis=1, keepdims=True)
    return jnp.broadcast_to(col, (L, L))


def kernel(
    h0_hbm, decay_hbm, steps_hbm, inc_hbm, coup_hbm, iw_hbm, gain_hbm, vw_hbm, gw_hbm,
    states_ref, read_ref,
    h0_ref, decay_ref, steps_ref, inc_ref, iw_ref, pack, incbuf, cbuf, vw, gw, gbuf, cth, ctl, xbuf, dc, sig, arow, prow, ns, na,
    dbuf, eb, tree, pref, msg, maps, starts, cols, stout, scout, stbuf, scbuf,
    local_sem, inc_ss, inc_rs, gain_ss, gain_rs, map_ss, map_rs, st_ss, st_rs,
):
    tm, blk = lax.axis_index("tm"), lax.axis_index("blk")
    seg, pos = tm // 8, lax.rem(tm, 8)
    flip = 4 * lax.rem(seg, 2)
    chain = lax.rem(pos + flip, 8)
    rec, lb = chain // 4, lax.rem(chain, 4)

    def holder(s):
        return (s * 8 + lax.rem(chain + 4 * lax.rem(s, 2), 8), blk)

    def near(i):
        dy, dz = AROUND[i]
        p = lax.rem(pos // 4 + dy, 2) * 4 + lax.rem(lax.rem(pos, 4) + dz, 4)
        return p, lax.rem(p + flip, 8)

    loads = [
        pltpu.make_async_copy(src, dst, local_sem.at[n])
        for n, (src, dst) in enumerate((
            (inc_hbm, inc_ref), (steps_hbm, steps_ref), (gain_hbm, gbuf.at[blk]), (decay_hbm, decay_ref),
            (iw_hbm, iw_ref), (h0_hbm, h0_ref), (coup_hbm.at[:, lb], cbuf), (vw_hbm, vw), (gw_hbm, gw)))
    ]
    load_inc, load_steps, load_gain, load_decay, load_iw, load_h0, load_c, load_v, load_g = loads
    for load in loads:
        load.start()
    barrier = pltpu.get_barrier_semaphore()
    for i in range(7):
        pl.semaphore_signal(barrier, inc=1, device_id=(seg * 8 + near(i)[0], blk), device_id_type=MESH)
    for i in range(8):
        pl.semaphore_signal(barrier, inc=1, device_id=(seg * 8 + near(i)[0], 1 - blk), device_id_type=MESH)

    def greet(s, _):
        pl.semaphore_signal(barrier, inc=1, device_id=holder(s), device_id_type=MESH)
        return 0

    lax.fori_loop(0, seg, greet, 0)
    load_inc.wait()
    load_steps.wait()

    for r in range(2):
        row = jnp.broadcast_to(steps_ref[r : r + 1, :], (16, 16))
        col = jnp.sum(jnp.where(iota((16, 16), 0) == iota((16, 16), 1), row, 0.0), axis=1, keepdims=True)
        pack[r, :, :] = jnp.zeros((16, L), F32)
        pack[r, :, 0:16] = inc_ref[r]
        pack[r, :, 16:17] = col
    load_gain.wait()

    pl.semaphore_wait(barrier, 15 + 7 - seg)

    def inc_copy(i):
        p, k = near(i)
        return pltpu.make_async_remote_copy(
            src_ref=pack.at[k // 4], dst_ref=incbuf.at[pl.ds(pos * 16, 16)], send_sem=inc_ss.at[p], recv_sem=inc_rs.at[pos],
            device_id=(seg * 8 + p, blk), device_id_type=MESH)

    def inc_arrival(i):
        p, k = near(i)
        return pltpu.make_async_remote_copy(
            src_ref=pack.at[k // 4], dst_ref=incbuf.at[pl.ds(p * 16, 16)], send_sem=inc_ss.at[p], recv_sem=inc_rs.at[p],
            device_id=(seg * 8 + p, blk), device_id_type=MESH)

    def gain_copy():
        return pltpu.make_async_remote_copy(
            src_ref=gbuf.at[blk], dst_ref=gbuf.at[blk], send_sem=gain_ss, recv_sem=gain_rs,
            device_id=(tm, 1 - blk), device_id_type=MESH)

    for i in range(7):
        inc_copy(i).start()
    gain_copy().start()
    incbuf[pl.ds(pl.multiple_of(pos * 16, 16), 16), :] = pack[rec]

    load_decay.wait()
    load_iw.wait()
    load_h0.wait()
    decay_row = decay_ref[pl.ds(lb, 1), :]
    dc[0:L, :] = -to_column(decay_row)
    dc[L:ROWS, :] = jnp.zeros((ROWS - L, L), F32)
    load_c.wait()
    for q in range(9):
        if q == 8:
            w = iw_ref[:, pl.ds(pl.multiple_of(lb * L, L), L)]
            wide = jnp.broadcast_to(w[:, None, :], (16, 8, L))
            first = jnp.where(iota((16, 8, L), 1) == 0, wide, 0.0).reshape(L, L)
            second = jnp.zeros((L, L), F32)
            for n, t in enumerate((first, second)):
                hi, lo = split2(t)
                cth[q, 0:L, n * L : (n + 1) * L] = hi
                cth[q, L : 2 * L, n * L : (n + 1) * L] = hi
                ctl[q, :, n * L : (n + 1) * L] = lo

    def transpose_pair(cp, _):
        a = cbuf[2 * cp].T.reshape(16, 8, L)
        b = cbuf[2 * cp + 1].T.reshape(16, 8, L)
        both = jnp.concatenate([a, b], axis=1)
        hi, lo = split2(both)
        base = pl.multiple_of(cp * 16, 16)
        for jb in range(16):
            q, n = jb // 2, jb % 2
            cth[q, pl.ds(base, 16), n * L : (n + 1) * L] = hi[jb]
            cth[q, pl.ds(base + L, 16), n * L : (n + 1) * L] = hi[jb]
            ctl[q, pl.ds(base, 16), n * L : (n + 1) * L] = lo[jb]
        return 0

    lax.fori_loop(0, 8, transpose_pair, 0)

    for i in range(7):
        inc_arrival(i).wait_recv()

    incp = jnp.concatenate([incbuf[pl.ds(l, 16, stride=8), :] for l in range(8)], axis=0)
    spread = (iota((L, L), 0) == iota((L, L), 1) // 8).astype(BF16)
    keep = (iota((8, L), 0) == lax.rem(iota((8, L), 1), 8))[None]
    for n, piece in enumerate(split2(incp)):
        wide = mm(piece, spread)
        x = jnp.where(keep, jnp.broadcast_to(wide[:, None, :], (L, 8, L)), 0.0)
        xbuf[:, n * L : (n + 1) * L] = x.reshape(8 * L, L).astype(BF16)

    stepbc = jnp.broadcast_to(incp[:, 16:17], (L, L))
    t_row, t_col = iota((L, L), 0), iota((L, L), 1)
    same = lax.rem(t_row, 16) == lax.rem(t_col, 16)
    sig[...] = exact_mask_sum((same & (t_col < t_row)).astype(BF16), stepbc)
    arow[...] = jnp.exp(-stepbc * decay_row)
    prow[...] = jnp.exp(-exact_mask_sum((same & (t_col <= t_row)).astype(BF16), stepbc) * decay_row)
    n_row, n_col = iota((NODES, L), 0), iota((NODES, L), 1)
    n_col = lax.rem(n_col, 16) * 8 + n_col // 16
    low, size = n_row * 8, 8 + 0 * n_row
    for first, width in ((16, 16), (24, 32), (28, 64), (30, 128)):
        low = jnp.where(n_row >= first, (n_row - first) * width, low)
        size = jnp.where(n_row >= first, width, size)
    low = jnp.where(n_row >= 32, 0, low)
    size = jnp.where(n_row >= 32, (n_row - 32) * 8, size)
    sums = exact_mask_sum(((n_col >= low) & (n_col < low + size)).astype(BF16), stepbc)
    ns[...] = sums
    na[...] = jnp.exp(-sums * decay_row)

    def compose(d1, n1, d2, n2):
        scale = jnp.exp(dc[...] * ns[n1 : n1 + 1, :])
        return scale * d2 + d1 * na[n2 : n2 + 1, :] + mm(d1.astype(BF16), d2[0:L].astype(BF16))

    first_of = (0, 16, 24, 28, 30)

    def node(level, i):
        return dbuf[7 * 16 + i] if level == 0 else tree[first_of[level] - 16 + i]

    def build(q, m):
        rows = 256
        x = xbuf[m * rows : (m + 1) * rows, :]
        e = mm(x, cth[q]) + mm(x[:, :L], ctl[q])
        nt = rows // 8
        t0, base = m * nt, q * 16
        s = sig[t0 : t0 + nt, :][:, None, :]
        pieces = []
        for n in range(2):
            en = e[:, n * L : (n + 1) * L].reshape(nt, 8, L)
            d = dc[base + 8 * n : base + 8 * n + 8, :][None]
            dbuf[t0 : t0 + nt, base + 8 * n : base + 8 * n + 8, :] = en * jnp.exp(d * s)
            pieces.append(en)
        eb[t0 : t0 + nt, base : base + 16, :] = jnp.concatenate(pieces, axis=1).astype(BF16)

    def advance(t):
        d = dbuf[t - 16]
        dbuf[t] = dbuf[t] + d * arow[t : t + 1, :] + mm(d.astype(BF16), eb[t, 0:L, :])

    waiting = []
    for m in range(4):
        for q in range(9):
            build(q, m)
            now = -(-len(waiting) // (9 - q))
            for t in waiting[:now]:
                advance(t)
            waiting = waiting[now:]
        waiting = list(range(max(16, 32 * m), 32 * m + 32))
    for t in waiting:
        advance(t)

    for level in range(1, 5):
        for i in range(16 >> level):
            tree[first_of[level] - 16 + i] = compose(
                node(level - 1, 2 * i), first_of[level - 1] + 2 * i,
                node(level - 1, 2 * i + 1), first_of[level - 1] + 2 * i + 1)

    whole = tree[14]
    init = h0_ref[:, pl.ds(pl.multiple_of(lb * L, L), L)]
    init = jnp.where(rec == 0, init[0:1], init[1:2])

    def apply_map(h, d_bf, a, v):
        hi, mid, lo = split3(h)
        rid = iota((16, L), 0)
        x = jnp.where(rid == 0, hi.astype(F32), jnp.where(rid == 1, mid.astype(F32), jnp.where(rid == 2, lo.astype(F32), 0.0)))
        return h * a + v + jnp.sum(mm(x.astype(BF16), d_bf), axis=0, keepdims=True)

    top = whole[0:L]
    a_all, v_all = na[30:31, :], whole[L : L + 1]
    msg[0:L, :] = top.astype(BF16)
    after = init * a_all + v_all + jnp.sum(to_column(init) * top, axis=0, keepdims=True)
    v_all = jnp.where(seg == 0, after, v_all)
    rid = iota((16, L), 0)
    tail = jnp.zeros((16, L), F32)
    for n, piece in enumerate(split3(a_all) + split3(v_all)):
        tail = jnp.where(rid == n, jnp.broadcast_to(piece.astype(F32), (16, L)), tail)
    msg[L:ROWS, :] = tail.astype(BF16)

    def map_copy(src, dst, rows):
        return pltpu.make_async_remote_copy(
            src_ref=msg.at[rows], dst_ref=maps.at[src, rows], send_sem=map_ss.at[dst], recv_sem=map_rs.at[src],
            device_id=holder(dst), device_id_type=MESH)

    full, last = pl.ds(0, ROWS), pl.ds(L, ROWS - L)

    def to_later(act):
        def one(n, _):
            @pl.when(seg == 0)
            def _():
                act(map_copy(seg, 7 - n, last))

            @pl.when(seg > 0)
            def _():
                act(map_copy(seg, 7 - n, full))

            return 0

        lax.fori_loop(0, 7 - seg, one, 0)

    to_later(lambda copy: copy.start())

    pref[0] = jnp.zeros((ROWS, L), F32)
    pref[1] = node(0, 0)
    pref[2] = node(1, 0)
    pref[4] = node(2, 0)
    pref[8] = node(3, 0)
    for dst, a, level, i in (
        (12, 8, 2, 2), (6, 4, 1, 2), (10, 8, 1, 4), (14, 12, 1, 6), (3, 2, 0, 2), (5, 4, 0, 4), (7, 6, 0, 6),
        (9, 8, 0, 8), (11, 10, 0, 10), (13, 12, 0, 12), (15, 14, 0, 14)):
        pref[dst] = compose(pref[a], 32 + a, node(level, i), first_of[level] + i)

    def tail_of(src):
        tail = maps[src, L:ROWS, :].astype(F32)
        return tail[0:1] + tail[1:2] + tail[2:3], tail[3:4] + tail[4:5] + tail[5:6]

    def begin():
        map_copy(0, 0, last).wait_recv()
        return tail_of(0)[1]

    def arrive(src, h):
        map_copy(src, src, full).wait_recv()
        a, v = tail_of(src)
        return apply_map(h, maps[src, 0:L, :], a, v)

    entry = lax.fori_loop(1, seg, arrive, lax.cond(seg > 0, begin, lambda: init))

    ones = (iota((16, L), 0) == 0).astype(F32)
    entry_col = jnp.concatenate([to_column(entry), ones], axis=0)

    def from_start(h, col, d, a):
        return h * a + jnp.sum(col * d, axis=0, keepdims=True)

    for g in range(16):
        hg = entry if g == 0 else from_start(entry, entry_col, pref[g], na[32 + g : 33 + g, :])
        starts[g, 0:1, :] = hg
        cols[g, 0:L, :] = to_column(hg)
        cols[g, L:ROWS, :] = ones

    def home(i, p, k):
        own = pltpu.make_async_remote_copy(
            src_ref=stout.at[p], dst_ref=stbuf.at[k], send_sem=st_ss.at[p], recv_sem=st_rs.at[k],
            device_id=(seg * 8 + p, blk), device_id_type=MESH)
        other = pltpu.make_async_remote_copy(
            src_ref=scout.at[p], dst_ref=scbuf.at[k], send_sem=st_ss.at[8 + p], recv_sem=st_rs.at[8 + k],
            device_id=(seg * 8 + p, 1 - blk), device_id_type=MESH)
        return (own, other) if i < 7 else (other,)

    gain_row = gbuf[blk, pl.ds(lb, 1), :]
    for i in range(8):
        p, _ = near(i)
        for half in range(2):
            g = 2 * p + half
            hg, col = starts[g, 0:1, :], cols[g]
            rows = []
            for l in range(8):
                t = l * 16 + g
                rows.append(from_start(hg, col, dbuf[t], prow[pl.ds(t, 1), :]))
            stout[p, half * 8 : half * 8 + 8, :] = jnp.concatenate(rows, axis=0)
        scout[p] = (stout[p] * gain_row).astype(BF16)
        for copy in home(i, p, chain):
            copy.start()
    stbuf[pl.ds(chain, 1)] = stout[pl.ds(pos, 1)]
    load_v.wait()
    load_g.wait()
    gain_copy().wait_recv()
    for i in range(8):
        p, k = near(i)
        for copy in home(i, p, k):
            copy.wait_recv()

    squares = jnp.zeros((32, 1), F32)
    mine, theirs = [], []
    other_gain = gbuf[1 - blk]
    for b in range(4):
        part = jnp.concatenate([stbuf[b], stbuf[4 + b]], axis=0)
        squares = squares + jnp.sum(part * part, axis=1, keepdims=True)
        mine.append((part * gbuf[blk, b : b + 1, :]).astype(BF16))
        part = jnp.concatenate([scbuf[b], scbuf[4 + b]], axis=0)
        theirs.append(part)
        part = part.astype(F32) / other_gain[b : b + 1]
        squares = squares + jnp.sum(part * part, axis=1, keepdims=True)
    mine, theirs = jnp.concatenate(mine, axis=1), jnp.concatenate(theirs, axis=1)
    first = blk == 0
    scaled = jnp.concatenate([jnp.where(first, mine, theirs), jnp.where(first, theirs, mine)], axis=1)
    inverse = lax.rsqrt(squares / UNITS + 1e-06)
    value = mm(scaled, vw[...]) * inverse
    gate = mm(scaled, gw[...]) * inverse
    out = (value * jax.nn.sigmoid(gate)).astype(BF16)
    read_ref[...] = out.reshape(2, 16, 512)
    for r in range(2):
        for b in range(4):
            states_ref[r, :, b * L : (b + 1) * L] = stbuf[4 * r + b]

    for i in range(7):
        inc_copy(i).wait_send()
    gain_copy().wait_send()

    to_later(lambda copy: copy.wait_send())
    for i in range(8):
        p, k = near(i)
        for copy in home(i, p, k):
            copy.wait_send()


def body(initial_state, decay_rate, step_sizes, increments, coupling, input_weight, gain, value_weight, gate_weight):
    args = (initial_state, decay_rate.reshape(4, L), step_sizes, increments, coupling, input_weight, gain.reshape(4, L),
            value_weight, gate_weight)
    args = [pltpu.with_memory_space_constraint(a, pltpu.HBM) for a in args]
    vmem, hbm = pl.BlockSpec(memory_space=pltpu.VMEM), pl.BlockSpec(memory_space=pltpu.HBM)
    dma = pltpu.SemaphoreType.DMA
    return pl.pallas_call(
        kernel,
        out_shape=(jax.ShapeDtypeStruct((2, 16, 512), F32), jax.ShapeDtypeStruct((2, 16, 512), BF16)),
        in_specs=[hbm] * 9,
        out_specs=(vmem, vmem),
        scratch_shapes=[
            pltpu.VMEM((2, 512), F32),
            pltpu.VMEM((4, L), F32),
            pltpu.VMEM((2, 16), F32),
            pltpu.VMEM((2, 16, 16), F32),
            pltpu.VMEM((16, 512), F32),
            pltpu.VMEM((2, 16, L), F32),
            pltpu.VMEM((L, L), F32),
            pltpu.VMEM((16, L, L), F32),
            pltpu.VMEM((1024, 512), BF16),
            pltpu.VMEM((1024, 512), BF16),
            pltpu.VMEM((2, 4, L), F32),
            pltpu.VMEM((9, 2 * L, 2 * L), BF16),
            pltpu.VMEM((9, L, 2 * L), BF16),
            pltpu.VMEM((8 * L, 2 * L), BF16),
            pltpu.VMEM((ROWS, L), F32),
            pltpu.VMEM((L, L), F32),
            pltpu.VMEM((L, L), F32),
            pltpu.VMEM((L, L), F32),
            pltpu.VMEM((NODES, L), F32),
            pltpu.VMEM((NODES, L), F32),
            pltpu.VMEM((L, ROWS, L), F32),
            pltpu.VMEM((L, ROWS, L), BF16),
            pltpu.VMEM((15, ROWS, L), F32),
            pltpu.VMEM((16, ROWS, L), F32),
            pltpu.VMEM((ROWS, L), BF16),
            pltpu.VMEM((8, ROWS, L), BF16),
            pltpu.VMEM((16, 8, L), F32),
            pltpu.VMEM((16, ROWS, L), F32),
            pltpu.VMEM((8, 16, L), F32),
            pltpu.VMEM((8, 16, L), BF16),
            pltpu.VMEM((8, 16, L), F32),
            pltpu.VMEM((8, 16, L), BF16),
            dma((9,)), dma((8,)), dma((8,)), dma, dma, dma((8,)), dma((8,)), dma((16,)), dma((16,)),
        ],
        compiler_params=pltpu.CompilerParams(
            collective_id=0, has_side_effects=True, vmem_limit_bytes=48 * 1024 * 1024),
        cost_estimate=pl.CostEstimate(flops=10**9, bytes_accessed=4 * 10**6, transcendentals=0),
    )(*args)


def solution(mesh):
    placed = (
        P(None, "blk"), P("blk"), P(None, "tm"), P(None, "tm", None), P(None, "blk", None, None),
        P(None, "blk"), P("blk"), P(None, "blk"), P(None, "blk"),
    )
    return jax.shard_map(
        body, mesh=mesh, in_specs=placed, out_specs=(P(None, "tm", "blk"), P(None, "tm", "blk")), check_vma=False)
```

```python
import functools

import jax
import jax.numpy as jnp
from jax import lax
from jax.experimental import pallas as pl
from jax.experimental.pallas import tpu as pltpu
from jax.sharding import PartitionSpec as P

MESH = pl.DeviceIdType.MESH
F32, BF16 = jnp.float32, jnp.bfloat16
UNITS = 1024
L = 128
ROWS = 144
NODES = 48
AROUND = ((1, 2), (0, 2), (1, 1), (1, 3), (0, 1), (0, 3), (1, 0), (0, 0))


def iota(shape, dim):
    return lax.broadcasted_iota(jnp.int32, shape, dim)


def split2(x):
    hi = x.astype(BF16)
    return hi, (x - hi.astype(F32)).astype(BF16)


def split3(x):
    hi = x.astype(BF16)
    rest = x - hi.astype(F32)
    mid = rest.astype(BF16)
    return hi, mid, (rest - mid.astype(F32)).astype(BF16)


def mm(a, b):
    return jnp.dot(a, b, preferred_element_type=F32)


def exact_mask_sum(mask, value):
    total = None
    for piece in split3(value):
        part = mm(mask, piece)
        total = part if total is None else total + part
    return total


def to_column(row):
    eye = iota((L, L), 0) == iota((L, L), 1)
    col = jnp.sum(jnp.where(eye, jnp.broadcast_to(row, (L, L)), 0.0), axis=1, keepdims=True)
    return jnp.broadcast_to(col, (L, L))


def kernel(
    h0_hbm, decay_hbm, steps_hbm, inc_hbm, coup_hbm, iw_hbm, gain_hbm, vw_hbm, gw_hbm,
    states_ref, read_ref,
    h0_ref, decay_ref, steps_ref, inc_ref, iw_ref, pack, incbuf, cbuf, vw, gw, gbuf, cth, xbuf, dc, sig, arow, prow, ns, na,
    dbuf, eb, tree, pref, msg, maps, starts, cols, stout, scout, stbuf, scbuf,
    local_sem, inc_ss, inc_rs, gain_ss, gain_rs, map_ss, map_rs, st_ss, st_rs,
):
    tm, blk = lax.axis_index("tm"), lax.axis_index("blk")
    seg, pos = tm // 8, lax.rem(tm, 8)
    flip = 4 * lax.rem(seg, 2)
    chain = lax.rem(pos + flip, 8)
    rec, lb = chain // 4, lax.rem(chain, 4)

    def holder(s):
        return (s * 8 + lax.rem(chain + 4 * lax.rem(s, 2), 8), blk)

    def near(i):
        dy, dz = AROUND[i]
        p = lax.rem(pos // 4 + dy, 2) * 4 + lax.rem(lax.rem(pos, 4) + dz, 4)
        return p, lax.rem(p + flip, 8)

    loads = [
        pltpu.make_async_copy(src, dst, local_sem.at[n])
        for n, (src, dst) in enumerate((
            (inc_hbm, inc_ref), (steps_hbm, steps_ref), (gain_hbm, gbuf.at[blk]), (decay_hbm, decay_ref),
            (iw_hbm, iw_ref), (h0_hbm, h0_ref), (coup_hbm.at[:, lb], cbuf), (vw_hbm, vw), (gw_hbm, gw)))
    ]
    load_inc, load_steps, load_gain, load_decay, load_iw, load_h0, load_c, load_v, load_g = loads
    for load in loads:
        load.start()
    barrier = pltpu.get_barrier_semaphore()
    for i in range(7):
        pl.semaphore_signal(barrier, inc=1, device_id=(seg * 8 + near(i)[0], blk), device_id_type=MESH)
    for i in range(8):
        pl.semaphore_signal(barrier, inc=1, device_id=(seg * 8 + near(i)[0], 1 - blk), device_id_type=MESH)

    def greet(s, _):
        pl.semaphore_signal(barrier, inc=1, device_id=holder(s), device_id_type=MESH)
        return 0

    lax.fori_loop(0, seg, greet, 0)
    load_inc.wait()
    load_steps.wait()

    for r in range(2):
        row = jnp.broadcast_to(steps_ref[r : r + 1, :], (16, 16))
        col = jnp.sum(jnp.where(iota((16, 16), 0) == iota((16, 16), 1), row, 0.0), axis=1, keepdims=True)
        pack[r, :, :] = jnp.zeros((16, L), F32)
        pack[r, :, 0:16] = inc_ref[r]
        pack[r, :, 16:17] = col
    load_gain.wait()

    pl.semaphore_wait(barrier, 15 + 7 - seg)

    def inc_copy(i):
        p, k = near(i)
        return pltpu.make_async_remote_copy(
            src_ref=pack.at[k // 4], dst_ref=incbuf.at[pl.ds(pos * 16, 16)], send_sem=inc_ss.at[p], recv_sem=inc_rs.at[pos],
            device_id=(seg * 8 + p, blk), device_id_type=MESH)

    def inc_arrival(i):
        p, k = near(i)
        return pltpu.make_async_remote_copy(
            src_ref=pack.at[k // 4], dst_ref=incbuf.at[pl.ds(p * 16, 16)], send_sem=inc_ss.at[p], recv_sem=inc_rs.at[p],
            device_id=(seg * 8 + p, blk), device_id_type=MESH)

    def gain_copy():
        return pltpu.make_async_remote_copy(
            src_ref=gbuf.at[blk], dst_ref=gbuf.at[blk], send_sem=gain_ss, recv_sem=gain_rs,
            device_id=(tm, 1 - blk), device_id_type=MESH)

    for i in range(7):
        inc_copy(i).start()
    gain_copy().start()
    incbuf[pl.ds(pl.multiple_of(pos * 16, 16), 16), :] = pack[rec]

    load_decay.wait()
    load_iw.wait()
    load_h0.wait()
    decay_row = decay_ref[pl.ds(lb, 1), :]
    dc[0:L, :] = -to_column(decay_row)
    dc[L:ROWS, :] = jnp.zeros((ROWS - L, L), F32)
    load_c.wait()
    drive = iw_ref[:, pl.ds(pl.multiple_of(lb * L, L), L)]
    drive = jnp.concatenate([drive, jnp.zeros((L - 16, L), F32)], axis=0)

    def transpose_pair(cp, _):
        a = cbuf[2 * cp].T.reshape(16, 8, L)
        b = cbuf[2 * cp + 1].T.reshape(16, 8, L)
        both = jnp.concatenate([a, b], axis=1)
        hi, lo = split2(both)
        base = pl.multiple_of(cp * 16, 16)
        for jb in range(16):
            q, n = jb // 2, jb % 2
            cth[q, pl.ds(base, 16), n * L : (n + 1) * L] = hi[jb]
            cth[q, pl.ds(base + L, 16), n * L : (n + 1) * L] = hi[jb]
            cth[q, pl.ds(base + 2 * L, 16), n * L : (n + 1) * L] = lo[jb]
        return 0

    lax.fori_loop(0, 8, transpose_pair, 0)

    for i in range(7):
        inc_arrival(i).wait_recv()

    incp = jnp.concatenate([incbuf[pl.ds(l, 16, stride=8), :] for l in range(8)], axis=0)
    spread = (iota((L, L), 0) == iota((L, L), 1) // 8).astype(BF16)
    keep = (iota((8, L), 0) == lax.rem(iota((8, L), 1), 8))[None]
    for n, piece in enumerate(split2(incp)):
        wide = mm(piece, spread)
        x = jnp.where(keep, jnp.broadcast_to(wide[:, None, :], (L, 8, L)), 0.0)
        x = x.reshape(8 * L, L).astype(BF16)
        xbuf[:, n * L : (n + 1) * L] = x
        if n == 0:
            xbuf[:, 2 * L : 3 * L] = x

    stepbc = jnp.broadcast_to(incp[:, 16:17], (L, L))
    t_row, t_col = iota((L, L), 0), iota((L, L), 1)
    same = lax.rem(t_row, 16) == lax.rem(t_col, 16)
    sig[...] = exact_mask_sum((same & (t_col < t_row)).astype(BF16), stepbc)
    arow[...] = jnp.exp(-stepbc * decay_row)
    prow[...] = jnp.exp(-exact_mask_sum((same & (t_col <= t_row)).astype(BF16), stepbc) * decay_row)
    n_row, n_col = iota((NODES, L), 0), iota((NODES, L), 1)
    n_col = lax.rem(n_col, 16) * 8 + n_col // 16
    low, size = n_row * 8, 8 + 0 * n_row
    for first, width in ((16, 16), (24, 32), (28, 64), (30, 128)):
        low = jnp.where(n_row >= first, (n_row - first) * width, low)
        size = jnp.where(n_row >= first, width, size)
    low = jnp.where(n_row >= 32, 0, low)
    size = jnp.where(n_row >= 32, (n_row - 32) * 8, size)
    sums = exact_mask_sum(((n_col >= low) & (n_col < low + size)).astype(BF16), stepbc)
    ns[...] = sums
    na[...] = jnp.exp(-sums * decay_row)

    def compose(d1, n1, d2, n2):
        scale = jnp.exp(dc[...] * ns[n1 : n1 + 1, :])
        return scale * d2 + d1 * na[n2 : n2 + 1, :] + mm(d1.astype(BF16), d2[0:L].astype(BF16))

    first_of = (0, 16, 24, 28, 30)

    def node(level, i):
        return dbuf[7 * 16 + i] if level == 0 else tree[first_of[level] - 16 + i]

    def build(q, m):
        rows = 512
        x = xbuf[m * rows : (m + 1) * rows, :]
        e = mm(x, cth[q])
        nt = rows // 8
        t0, base = m * nt, q * 16
        s = sig[t0 : t0 + nt, :][:, None, :]
        pieces = []
        for n in range(2):
            en = e[:, n * L : (n + 1) * L].reshape(nt, 8, L)
            d = dc[base + 8 * n : base + 8 * n + 8, :][None]
            dbuf[t0 : t0 + nt, base + 8 * n : base + 8 * n + 8, :] = en * jnp.exp(d * s)
            pieces.append(en)
        eb[t0 : t0 + nt, base : base + 16, :] = jnp.concatenate(pieces, axis=1).astype(BF16)

    def advance(t):
        d = dbuf[t - 16]
        dbuf[t] = dbuf[t] + d * arow[t : t + 1, :] + mm(d.astype(BF16), eb[t])

    inc_hi, inc_lo = split2(jnp.where(t_col < 16, incp, 0.0))
    drive_hi, drive_lo = split2(drive)
    vector = mm(inc_hi, drive_hi) + mm(inc_lo, drive_hi) + mm(inc_hi, drive_lo)
    dbuf[:, L : L + 8, :] = jnp.where(iota((L, 8, L), 1) == 0, jnp.broadcast_to(vector[:, None, :], (L, 8, L)), 0.0)
    dbuf[:, L + 8 : ROWS, :] = jnp.zeros((L, 8, L), F32)

    waiting = []
    for m in range(2):
        for q in range(8):
            build(q, m)
            now = -(-len(waiting) // (8 - q))
            for t in waiting[:now]:
                advance(t)
            waiting = waiting[now:]
        waiting = list(range(max(16, 64 * m), 64 * m + 64))
    for t in waiting:
        advance(t)

    for level in range(1, 5):
        for i in range(16 >> level):
            tree[first_of[level] - 16 + i] = compose(
                node(level - 1, 2 * i), first_of[level - 1] + 2 * i,
                node(level - 1, 2 * i + 1), first_of[level - 1] + 2 * i + 1)

    whole = tree[14]
    init = h0_ref[:, pl.ds(pl.multiple_of(lb * L, L), L)]
    init = jnp.where(rec == 0, init[0:1], init[1:2])

    def apply_map(h, d_bf, a, v):
        hi, mid, lo = split3(h)
        rid = iota((16, L), 0)
        x = jnp.where(rid == 0, hi.astype(F32), jnp.where(rid == 1, mid.astype(F32), jnp.where(rid == 2, lo.astype(F32), 0.0)))
        return h * a + v + jnp.sum(mm(x.astype(BF16), d_bf), axis=0, keepdims=True)

    top = whole[0:L]
    a_all, v_all = na[30:31, :], whole[L : L + 1]
    msg[0:L, :] = top.astype(BF16)
    after = init * a_all + v_all + jnp.sum(to_column(init) * top, axis=0, keepdims=True)
    v_all = jnp.where(seg == 0, after, v_all)
    rid = iota((16, L), 0)
    tail = jnp.zeros((16, L), F32)
    for n, piece in enumerate(split3(a_all) + split3(v_all)):
        tail = jnp.where(rid == n, jnp.broadcast_to(piece.astype(F32), (16, L)), tail)
    msg[L:ROWS, :] = tail.astype(BF16)

    def map_copy(src, dst, rows):
        return pltpu.make_async_remote_copy(
            src_ref=msg.at[rows], dst_ref=maps.at[src, rows], send_sem=map_ss.at[dst], recv_sem=map_rs.at[src],
            device_id=holder(dst), device_id_type=MESH)

    full, last = pl.ds(0, ROWS), pl.ds(L, ROWS - L)

    def to_later(act):
        def one(n, _):
            @pl.when(seg == 0)
            def _():
                act(map_copy(seg, 7 - n, last))

            @pl.when(seg > 0)
            def _():
                act(map_copy(seg, 7 - n, full))

            return 0

        lax.fori_loop(0, 7 - seg, one, 0)

    to_later(lambda copy: copy.start())

    pref[0] = jnp.zeros((ROWS, L), F32)
    pref[1] = node(0, 0)
    pref[2] = node(1, 0)
    pref[4] = node(2, 0)
    pref[8] = node(3, 0)
    for dst, a, level, i in (
        (12, 8, 2, 2), (6, 4, 1, 2), (10, 8, 1, 4), (14, 12, 1, 6), (3, 2, 0, 2), (5, 4, 0, 4), (7, 6, 0, 6),
        (9, 8, 0, 8), (11, 10, 0, 10), (13, 12, 0, 12), (15, 14, 0, 14)):
        pref[dst] = compose(pref[a], 32 + a, node(level, i), first_of[level] + i)

    def tail_of(src):
        tail = maps[src, L:ROWS, :].astype(F32)
        return tail[0:1] + tail[1:2] + tail[2:3], tail[3:4] + tail[4:5] + tail[5:6]

    def begin():
        map_copy(0, 0, last).wait_recv()
        return tail_of(0)[1]

    def arrive(src, h):
        map_copy(src, src, full).wait_recv()
        a, v = tail_of(src)
        return apply_map(h, maps[src, 0:L, :], a, v)

    entry = lax.fori_loop(1, seg, arrive, lax.cond(seg > 0, begin, lambda: init))

    ones = (iota((16, L), 0) == 0).astype(F32)
    entry_col = jnp.concatenate([to_column(entry), ones], axis=0)

    def from_start(h, col, d, a):
        return h * a + jnp.sum(col * d, axis=0, keepdims=True)

    for g in range(16):
        hg = entry if g == 0 else from_start(entry, entry_col, pref[g], na[32 + g : 33 + g, :])
        starts[g, 0:1, :] = hg
        cols[g, 0:L, :] = to_column(hg)
        cols[g, L:ROWS, :] = ones

    def home(i, p, k):
        own = pltpu.make_async_remote_copy(
            src_ref=stout.at[p], dst_ref=stbuf.at[k], send_sem=st_ss.at[p], recv_sem=st_rs.at[k],
            device_id=(seg * 8 + p, blk), device_id_type=MESH)
        other = pltpu.make_async_remote_copy(
            src_ref=scout.at[p], dst_ref=scbuf.at[k], send_sem=st_ss.at[8 + p], recv_sem=st_rs.at[8 + k],
            device_id=(seg * 8 + p, 1 - blk), device_id_type=MESH)
        return (own, other) if i < 7 else (other,)

    gain_row = gbuf[blk, pl.ds(lb, 1), :]
    for i in range(8):
        p, _ = near(i)
        for half in range(2):
            g = 2 * p + half
            hg, col = starts[g, 0:1, :], cols[g]
            rows = []
            for l in range(8):
                t = l * 16 + g
                rows.append(from_start(hg, col, dbuf[t], prow[pl.ds(t, 1), :]))
            stout[p, half * 8 : half * 8 + 8, :] = jnp.concatenate(rows, axis=0)
        scout[p] = (stout[p] * gain_row).astype(BF16)
        for copy in home(i, p, chain):
            copy.start()
    stbuf[pl.ds(chain, 1)] = stout[pl.ds(pos, 1)]
    load_v.wait()
    load_g.wait()
    gain_copy().wait_recv()
    for i in range(8):
        p, k = near(i)
        for copy in home(i, p, k):
            copy.wait_recv()

    squares = jnp.zeros((32, 1), F32)
    mine, theirs = [], []
    other_gain = gbuf[1 - blk]
    for b in range(4):
        part = jnp.concatenate([stbuf[b], stbuf[4 + b]], axis=0)
        squares = squares + jnp.sum(part * part, axis=1, keepdims=True)
        mine.append((part * gbuf[blk, b : b + 1, :]).astype(BF16))
        part = jnp.concatenate([scbuf[b], scbuf[4 + b]], axis=0)
        theirs.append(part)
        part = part.astype(F32) / other_gain[b : b + 1]
        squares = squares + jnp.sum(part * part, axis=1, keepdims=True)
    mine, theirs = jnp.concatenate(mine, axis=1), jnp.concatenate(theirs, axis=1)
    first = blk == 0
    scaled = jnp.concatenate([jnp.where(first, mine, theirs), jnp.where(first, theirs, mine)], axis=1)
    inverse = lax.rsqrt(squares / UNITS + 1e-06)
    value = mm(scaled, vw[...]) * inverse
    gate = mm(scaled, gw[...]) * inverse
    out = (value * jax.nn.sigmoid(gate)).astype(BF16)
    read_ref[...] = out.reshape(2, 16, 512)
    for r in range(2):
        for b in range(4):
            states_ref[r, :, b * L : (b + 1) * L] = stbuf[4 * r + b]

    for i in range(7):
        inc_copy(i).wait_send()
    gain_copy().wait_send()

    to_later(lambda copy: copy.wait_send())
    for i in range(8):
        p, k = near(i)
        for copy in home(i, p, k):
            copy.wait_send()


def deliver(a_ref, b_ref, x_ref, y_ref, sem):
    copies = [pltpu.make_async_copy(a_ref, x_ref, sem.at[0]), pltpu.make_async_copy(b_ref, y_ref, sem.at[1])]
    for copy in copies:
        copy.start()
    for copy in copies:
        copy.wait()


def body(initial_state, decay_rate, step_sizes, increments, coupling, input_weight, gain, value_weight, gate_weight):
    args = (initial_state, decay_rate.reshape(4, L), step_sizes, increments, coupling, input_weight, gain.reshape(4, L),
            value_weight, gate_weight)
    args = [pltpu.with_memory_space_constraint(a, pltpu.HBM) for a in args]
    vmem, hbm = pl.BlockSpec(memory_space=pltpu.VMEM), pl.BlockSpec(memory_space=pltpu.HBM)
    dma = pltpu.SemaphoreType.DMA
    parts = pl.pallas_call(
        kernel,
        out_shape=(jax.ShapeDtypeStruct((2, 16, 512), F32), jax.ShapeDtypeStruct((2, 16, 512), BF16)),
        in_specs=[hbm] * 9,
        out_specs=(vmem, vmem),
        scratch_shapes=[
            pltpu.VMEM((2, 512), F32),
            pltpu.VMEM((4, L), F32),
            pltpu.VMEM((2, 16), F32),
            pltpu.VMEM((2, 16, 16), F32),
            pltpu.VMEM((16, 512), F32),
            pltpu.VMEM((2, 16, L), F32),
            pltpu.VMEM((L, L), F32),
            pltpu.VMEM((16, L, L), F32),
            pltpu.VMEM((1024, 512), BF16),
            pltpu.VMEM((1024, 512), BF16),
            pltpu.VMEM((2, 4, L), F32),
            pltpu.VMEM((8, 3 * L, 2 * L), BF16),
            pltpu.VMEM((8 * L, 3 * L), BF16),
            pltpu.VMEM((ROWS, L), F32),
            pltpu.VMEM((L, L), F32),
            pltpu.VMEM((L, L), F32),
            pltpu.VMEM((L, L), F32),
            pltpu.VMEM((NODES, L), F32),
            pltpu.VMEM((NODES, L), F32),
            pltpu.VMEM((L, ROWS, L), F32),
            pltpu.VMEM((L, L, L), BF16),
            pltpu.VMEM((15, ROWS, L), F32),
            pltpu.VMEM((16, ROWS, L), F32),
            pltpu.VMEM((ROWS, L), BF16),
            pltpu.VMEM((8, ROWS, L), BF16),
            pltpu.VMEM((16, 8, L), F32),
            pltpu.VMEM((16, ROWS, L), F32),
            pltpu.VMEM((8, 16, L), F32),
            pltpu.VMEM((8, 16, L), BF16),
            pltpu.VMEM((8, 16, L), F32),
            pltpu.VMEM((8, 16, L), BF16),
            dma((9,)), dma((8,)), dma((8,)), dma, dma, dma((8,)), dma((8,)), dma((16,)), dma((16,)),
        ],
        compiler_params=pltpu.CompilerParams(
            collective_id=0, has_side_effects=True, vmem_limit_bytes=48 * 1024 * 1024),
        cost_estimate=pl.CostEstimate(flops=10**9, bytes_accessed=4 * 10**6, transcendentals=0),
    )(*args)
    anywhere = pl.BlockSpec(memory_space=pl.ANY)
    return pl.pallas_call(
        deliver,
        out_shape=(jax.ShapeDtypeStruct((2, 16, 512), F32), jax.ShapeDtypeStruct((2, 16, 512), BF16)),
        in_specs=[anywhere] * 2,
        out_specs=(hbm, hbm),
        scratch_shapes=[dma((2,))],
        compiler_params=pltpu.CompilerParams(vmem_limit_bytes=1024 * 1024),
    )(*parts)


def solution(mesh):
    placed = (
        P(None, "blk"), P("blk"), P(None, "tm"), P(None, "tm", None), P(None, "blk", None, None),
        P(None, "blk"), P("blk"), P(None, "blk"), P(None, "blk"),
    )
    return jax.shard_map(
        body, mesh=mesh, in_specs=placed, out_specs=(P(None, "tm", "blk"), P(None, "tm", "blk")), check_vma=False)
```

```python
import functools

import jax
import jax.numpy as jnp
from jax import lax
from jax.experimental import pallas as pl
from jax.experimental.pallas import tpu as pltpu
from jax.sharding import PartitionSpec as P

MESH = pl.DeviceIdType.MESH
F32, BF16 = jnp.float32, jnp.bfloat16
UNITS = 1024
L = 128
ROWS = 144
NODES = 48
AROUND = ((1, 2), (0, 2), (1, 1), (1, 3), (0, 1), (0, 3), (1, 0), (0, 0))


def iota(shape, dim):
    return lax.broadcasted_iota(jnp.int32, shape, dim)


def split2(x):
    hi = x.astype(BF16)
    return hi, (x - hi.astype(F32)).astype(BF16)


def split3(x):
    hi = x.astype(BF16)
    rest = x - hi.astype(F32)
    mid = rest.astype(BF16)
    return hi, mid, (rest - mid.astype(F32)).astype(BF16)


def mm(a, b):
    return jnp.dot(a, b, preferred_element_type=F32)


def exact_mask_sum(mask, value):
    total = None
    for piece in split3(value):
        part = mm(mask, piece)
        total = part if total is None else total + part
    return total


def to_column(row):
    eye = iota((L, L), 0) == iota((L, L), 1)
    col = jnp.sum(jnp.where(eye, jnp.broadcast_to(row, (L, L)), 0.0), axis=1, keepdims=True)
    return jnp.broadcast_to(col, (L, L))


def kernel(
    h0_hbm, decay_hbm, steps_hbm, inc_hbm, coup_hbm, iw_hbm, gain_hbm, vw_hbm, gw_hbm,
    states_ref, read_ref,
    h0_ref, decay_ref, steps_ref, inc_ref, iw_ref, pack, incbuf, cbuf, vw, gw, gbuf, cth, xbuf, dc, sig, arow, prow, ns, na,
    dbuf, eb, tree, pref, msg, maps, starts, cols, stout, scout, stbuf, scbuf,
    local_sem, inc_ss, inc_rs, gain_ss, gain_rs, map_ss, map_rs, st_ss, st_rs,
):
    tm, blk = lax.axis_index("tm"), lax.axis_index("blk")
    seg, pos = tm // 8, lax.rem(tm, 8)
    flip = 4 * lax.rem(seg, 2)
    chain = lax.rem(pos + flip, 8)
    rec, lb = chain // 4, lax.rem(chain, 4)

    def holder(s):
        return (s * 8 + lax.rem(chain + 4 * lax.rem(s, 2), 8), blk)

    def near(i):
        dy, dz = AROUND[i]
        p = lax.rem(pos // 4 + dy, 2) * 4 + lax.rem(lax.rem(pos, 4) + dz, 4)
        return p, lax.rem(p + flip, 8)

    loads = [
        pltpu.make_async_copy(src, dst, local_sem.at[n])
        for n, (src, dst) in enumerate((
            (inc_hbm, inc_ref), (steps_hbm, steps_ref), (gain_hbm, gbuf.at[blk]), (decay_hbm, decay_ref),
            (iw_hbm, iw_ref), (h0_hbm, h0_ref), (coup_hbm.at[:, lb], cbuf), (vw_hbm, vw), (gw_hbm, gw)))
    ]
    load_inc, load_steps, load_gain, load_decay, load_iw, load_h0, load_c, load_v, load_g = loads
    for load in loads:
        load.start()
    barrier = pltpu.get_barrier_semaphore()
    for i in range(7):
        pl.semaphore_signal(barrier, inc=1, device_id=(seg * 8 + near(i)[0], blk), device_id_type=MESH)
    for i in range(8):
        pl.semaphore_signal(barrier, inc=1, device_id=(seg * 8 + near(i)[0], 1 - blk), device_id_type=MESH)

    def greet(s, _):
        pl.semaphore_signal(barrier, inc=1, device_id=holder(s), device_id_type=MESH)
        return 0

    lax.fori_loop(0, seg, greet, 0)
    load_inc.wait()
    load_steps.wait()

    for r in range(2):
        row = jnp.broadcast_to(steps_ref[r : r + 1, :], (16, 16))
        col = jnp.sum(jnp.where(iota((16, 16), 0) == iota((16, 16), 1), row, 0.0), axis=1, keepdims=True)
        pack[r, :, :] = jnp.zeros((16, L), F32)
        pack[r, :, 0:16] = inc_ref[r]
        pack[r, :, 16:17] = col
    load_gain.wait()

    pl.semaphore_wait(barrier, 15 + 7 - seg)

    def inc_copy(i):
        p, k = near(i)
        return pltpu.make_async_remote_copy(
            src_ref=pack.at[k // 4], dst_ref=incbuf.at[pl.ds(pos * 16, 16)], send_sem=inc_ss.at[p], recv_sem=inc_rs.at[pos],
            device_id=(seg * 8 + p, blk), device_id_type=MESH)

    def inc_arrival(i):
        p, k = near(i)
        return pltpu.make_async_remote_copy(
            src_ref=pack.at[k // 4], dst_ref=incbuf.at[pl.ds(p * 16, 16)], send_sem=inc_ss.at[p], recv_sem=inc_rs.at[p],
            device_id=(seg * 8 + p, blk), device_id_type=MESH)

    def gain_copy():
        return pltpu.make_async_remote_copy(
            src_ref=gbuf.at[blk], dst_ref=gbuf.at[blk], send_sem=gain_ss, recv_sem=gain_rs,
            device_id=(tm, 1 - blk), device_id_type=MESH)

    for i in range(7):
        inc_copy(i).start()
    gain_copy().start()
    incbuf[pl.ds(pl.multiple_of(pos * 16, 16), 16), :] = pack[rec]

    load_decay.wait()
    load_iw.wait()
    load_h0.wait()
    decay_row = decay_ref[pl.ds(lb, 1), :]
    dc[0:L, :] = -to_column(decay_row)
    dc[L:ROWS, :] = jnp.zeros((ROWS - L, L), F32)
    load_c.wait()
    drive = iw_ref[:, pl.ds(pl.multiple_of(lb * L, L), L)]
    drive = jnp.concatenate([drive, jnp.zeros((L - 16, L), F32)], axis=0)

    def transpose_pair(cp, _):
        a = cbuf[2 * cp].T.reshape(16, 8, L)
        b = cbuf[2 * cp + 1].T.reshape(16, 8, L)
        both = jnp.concatenate([a, b], axis=1)
        hi, lo = split2(both)
        base = pl.multiple_of(cp * 16, 16)
        for jb in range(16):
            q, n = jb // 2, jb % 2
            cth[q, pl.ds(base, 16), n * L : (n + 1) * L] = hi[jb]
            cth[q, pl.ds(base + L, 16), n * L : (n + 1) * L] = hi[jb]
            cth[q, pl.ds(base + 2 * L, 16), n * L : (n + 1) * L] = lo[jb]
        return 0

    lax.fori_loop(0, 8, transpose_pair, 0)

    for i in range(7):
        inc_arrival(i).wait_recv()

    incp = jnp.concatenate([incbuf[pl.ds(l, 16, stride=8), :] for l in range(8)], axis=0)
    spread = (iota((L, L), 0) == iota((L, L), 1) // 8).astype(BF16)
    keep = (iota((8, L), 0) == lax.rem(iota((8, L), 1), 8))[None]
    for n, piece in enumerate(split2(incp)):
        wide = mm(piece, spread)
        x = jnp.where(keep, jnp.broadcast_to(wide[:, None, :], (L, 8, L)), 0.0)
        x = x.reshape(8 * L, L).astype(BF16)
        xbuf[:, n * L : (n + 1) * L] = x
        if n == 0:
            xbuf[:, 2 * L : 3 * L] = x

    stepbc = jnp.broadcast_to(incp[:, 16:17], (L, L))
    t_row, t_col = iota((L, L), 0), iota((L, L), 1)
    same = lax.rem(t_row, 16) == lax.rem(t_col, 16)
    sig[...] = exact_mask_sum((same & (t_col < t_row)).astype(BF16), stepbc)
    arow[...] = jnp.exp(-stepbc * decay_row)
    prow[...] = jnp.exp(-exact_mask_sum((same & (t_col <= t_row)).astype(BF16), stepbc) * decay_row)
    n_row, n_col = iota((NODES, L), 0), iota((NODES, L), 1)
    n_col = lax.rem(n_col, 16) * 8 + n_col // 16
    low, size = n_row * 8, 8 + 0 * n_row
    for first, width in ((16, 16), (24, 32), (28, 64), (30, 128)):
        low = jnp.where(n_row >= first, (n_row - first) * width, low)
        size = jnp.where(n_row >= first, width, size)
    low = jnp.where(n_row >= 32, 0, low)
    size = jnp.where(n_row >= 32, (n_row - 32) * 8, size)
    sums = exact_mask_sum(((n_col >= low) & (n_col < low + size)).astype(BF16), stepbc)
    ns[...] = sums
    na[...] = jnp.exp(-sums * decay_row)

    def compose(d1, n1, d2, n2):
        scale = jnp.exp(dc[...] * ns[n1 : n1 + 1, :])
        return scale * d2 + d1 * na[n2 : n2 + 1, :] + mm(d1.astype(BF16), d2[0:L].astype(BF16))

    first_of = (0, 16, 24, 28, 30)

    def node(level, i):
        return dbuf[7 * 16 + i] if level == 0 else tree[first_of[level] - 16 + i]

    def build(q, m):
        rows = 512
        x = xbuf[m * rows : (m + 1) * rows, :]
        e = mm(x, cth[q])
        nt = rows // 8
        t0, base = m * nt, q * 16
        s = sig[t0 : t0 + nt, :][:, None, :]
        pieces = []
        for n in range(2):
            en = e[:, n * L : (n + 1) * L].reshape(nt, 8, L)
            d = dc[base + 8 * n : base + 8 * n + 8, :][None]
            dbuf[t0 : t0 + nt, base + 8 * n : base + 8 * n + 8, :] = en * jnp.exp(d * s)
            pieces.append(en)
        eb[t0 : t0 + nt, base : base + 16, :] = jnp.concatenate(pieces, axis=1).astype(BF16)

    def advance(t):
        d = dbuf[t - 16]
        dbuf[t] = dbuf[t] + d * arow[t : t + 1, :] + mm(d.astype(BF16), eb[t])

    inc_hi, inc_lo = split2(jnp.where(t_col < 16, incp, 0.0))
    drive_hi, drive_lo = split2(drive)
    vector = mm(inc_hi, drive_hi) + mm(inc_lo, drive_hi) + mm(inc_hi, drive_lo)
    dbuf[:, L : L + 8, :] = jnp.where(iota((L, 8, L), 1) == 0, jnp.broadcast_to(vector[:, None, :], (L, 8, L)), 0.0)
    dbuf[:, L + 8 : ROWS, :] = jnp.zeros((L, 8, L), F32)

    waiting = []
    for m in range(2):
        for q in range(8):
            build(q, m)
            now = -(-len(waiting) // (8 - q))
            for t in waiting[:now]:
                advance(t)
            waiting = waiting[now:]
        waiting = list(range(max(16, 64 * m), 64 * m + 64))
    for t in waiting:
        advance(t)

    for level in range(1, 5):
        for i in range(16 >> level):
            tree[first_of[level] - 16 + i] = compose(
                node(level - 1, 2 * i), first_of[level - 1] + 2 * i,
                node(level - 1, 2 * i + 1), first_of[level - 1] + 2 * i + 1)

    whole = tree[14]
    init = h0_ref[:, pl.ds(pl.multiple_of(lb * L, L), L)]
    init = jnp.where(rec == 0, init[0:1], init[1:2])

    def apply_map(h, d_bf, a, v):
        hi, mid, lo = split3(h)
        rid = iota((16, L), 0)
        x = jnp.where(rid == 0, hi.astype(F32), jnp.where(rid == 1, mid.astype(F32), jnp.where(rid == 2, lo.astype(F32), 0.0)))
        return h * a + v + jnp.sum(mm(x.astype(BF16), d_bf), axis=0, keepdims=True)

    top = whole[0:L]
    a_all, v_all = na[30:31, :], whole[L : L + 1]
    msg[0:L, :] = top.astype(BF16)
    after = init * a_all + v_all + jnp.sum(to_column(init) * top, axis=0, keepdims=True)
    v_all = jnp.where(seg == 0, after, v_all)
    rid = iota((16, L), 0)
    tail = jnp.zeros((16, L), F32)
    for n, piece in enumerate(split3(a_all) + split3(v_all)):
        tail = jnp.where(rid == n, jnp.broadcast_to(piece.astype(F32), (16, L)), tail)
    msg[L:ROWS, :] = tail.astype(BF16)

    def map_copy(src, dst, rows):
        return pltpu.make_async_remote_copy(
            src_ref=msg.at[rows], dst_ref=maps.at[src, rows], send_sem=map_ss.at[dst], recv_sem=map_rs.at[src],
            device_id=holder(dst), device_id_type=MESH)

    full, last = pl.ds(0, ROWS), pl.ds(L, ROWS - L)

    def to_later(act):
        def one(n, _):
            @pl.when(seg == 0)
            def _():
                act(map_copy(seg, seg + 1 + n, last))

            @pl.when(seg > 0)
            def _():
                act(map_copy(seg, seg + 1 + n, full))

            return 0

        lax.fori_loop(0, 7 - seg, one, 0)

    to_later(lambda copy: copy.start())

    pref[0] = jnp.zeros((ROWS, L), F32)
    pref[1] = node(0, 0)
    pref[2] = node(1, 0)
    pref[4] = node(2, 0)
    pref[8] = node(3, 0)
    for dst, a, level, i in (
        (12, 8, 2, 2), (6, 4, 1, 2), (10, 8, 1, 4), (14, 12, 1, 6), (3, 2, 0, 2), (5, 4, 0, 4), (7, 6, 0, 6),
        (9, 8, 0, 8), (11, 10, 0, 10), (13, 12, 0, 12), (15, 14, 0, 14)):
        pref[dst] = compose(pref[a], 32 + a, node(level, i), first_of[level] + i)

    def tail_of(src):
        tail = maps[src, L:ROWS, :].astype(F32)
        return tail[0:1] + tail[1:2] + tail[2:3], tail[3:4] + tail[4:5] + tail[5:6]

    def begin():
        map_copy(0, 0, last).wait_recv()
        return tail_of(0)[1]

    def arrive(src, h):
        map_copy(src, src, full).wait_recv()
        a, v = tail_of(src)
        return apply_map(h, maps[src, 0:L, :], a, v)

    entry = lax.fori_loop(1, seg, arrive, lax.cond(seg > 0, begin, lambda: init))

    ones = (iota((16, L), 0) == 0).astype(F32)
    entry_col = jnp.concatenate([to_column(entry), ones], axis=0)

    def from_start(h, col, d, a):
        return h * a + jnp.sum(col * d, axis=0, keepdims=True)

    for g in range(16):
        hg = entry if g == 0 else from_start(entry, entry_col, pref[g], na[32 + g : 33 + g, :])
        starts[g, 0:1, :] = hg
        cols[g, 0:L, :] = to_column(hg)
        cols[g, L:ROWS, :] = ones

    def home(i, p, k):
        own = pltpu.make_async_remote_copy(
            src_ref=stout.at[p], dst_ref=stbuf.at[k], send_sem=st_ss.at[p], recv_sem=st_rs.at[k],
            device_id=(seg * 8 + p, blk), device_id_type=MESH)
        other = pltpu.make_async_remote_copy(
            src_ref=scout.at[p], dst_ref=scbuf.at[k], send_sem=st_ss.at[8 + p], recv_sem=st_rs.at[8 + k],
            device_id=(seg * 8 + p, 1 - blk), device_id_type=MESH)
        return (own, other) if i < 7 else (other,)

    gain_row = gbuf[blk, pl.ds(lb, 1), :]
    for i in range(8):
        p, _ = near(i)
        for half in range(2):
            g = 2 * p + half
            hg, col = starts[g, 0:1, :], cols[g]
            rows = []
            for l in range(8):
                t = l * 16 + g
                rows.append(from_start(hg, col, dbuf[t], prow[pl.ds(t, 1), :]))
            stout[p, half * 8 : half * 8 + 8, :] = jnp.concatenate(rows, axis=0)
        scout[p] = (stout[p] * gain_row).astype(BF16)
        for copy in home(i, p, chain):
            copy.start()
    stbuf[pl.ds(chain, 1)] = stout[pl.ds(pos, 1)]
    load_v.wait()
    load_g.wait()
    gain_copy().wait_recv()
    for i in range(8):
        p, k = near(i)
        for copy in home(i, p, k):
            copy.wait_recv()

    squares = jnp.zeros((32, 1), F32)
    mine, theirs = [], []
    other_gain = gbuf[1 - blk]
    for b in range(4):
        part = jnp.concatenate([stbuf[b], stbuf[4 + b]], axis=0)
        squares = squares + jnp.sum(part * part, axis=1, keepdims=True)
        mine.append((part * gbuf[blk, b : b + 1, :]).astype(BF16))
        part = jnp.concatenate([scbuf[b], scbuf[4 + b]], axis=0)
        theirs.append(part)
        part = part.astype(F32) / other_gain[b : b + 1]
        squares = squares + jnp.sum(part * part, axis=1, keepdims=True)
    mine, theirs = jnp.concatenate(mine, axis=1), jnp.concatenate(theirs, axis=1)
    first = blk == 0
    scaled = jnp.concatenate([jnp.where(first, mine, theirs), jnp.where(first, theirs, mine)], axis=1)
    inverse = lax.rsqrt(squares / UNITS + 1e-06)
    value = mm(scaled, vw[...]) * inverse
    gate = mm(scaled, gw[...]) * inverse
    out = (value * jax.nn.sigmoid(gate)).astype(BF16)
    read_ref[...] = out.reshape(2, 16, 512)
    for r in range(2):
        for b in range(4):
            states_ref[r, :, b * L : (b + 1) * L] = stbuf[4 * r + b]

    for i in range(7):
        inc_copy(i).wait_send()
    gain_copy().wait_send()

    to_later(lambda copy: copy.wait_send())
    for i in range(8):
        p, k = near(i)
        for copy in home(i, p, k):
            copy.wait_send()


def deliver(a_ref, b_ref, x_ref, y_ref, sem):
    copies = [pltpu.make_async_copy(a_ref, x_ref, sem.at[0]), pltpu.make_async_copy(b_ref, y_ref, sem.at[1])]
    for copy in copies:
        copy.start()
    for copy in copies:
        copy.wait()


def body(initial_state, decay_rate, step_sizes, increments, coupling, input_weight, gain, value_weight, gate_weight):
    args = (initial_state, decay_rate.reshape(4, L), step_sizes, increments, coupling, input_weight, gain.reshape(4, L),
            value_weight, gate_weight)
    args = [pltpu.with_memory_space_constraint(a, pltpu.HBM) for a in args]
    vmem, hbm = pl.BlockSpec(memory_space=pltpu.VMEM), pl.BlockSpec(memory_space=pltpu.HBM)
    dma = pltpu.SemaphoreType.DMA
    parts = pl.pallas_call(
        kernel,
        out_shape=(jax.ShapeDtypeStruct((2, 16, 512), F32), jax.ShapeDtypeStruct((2, 16, 512), BF16)),
        in_specs=[hbm] * 9,
        out_specs=(vmem, vmem),
        scratch_shapes=[
            pltpu.VMEM((2, 512), F32),
            pltpu.VMEM((4, L), F32),
            pltpu.VMEM((2, 16), F32),
            pltpu.VMEM((2, 16, 16), F32),
            pltpu.VMEM((16, 512), F32),
            pltpu.VMEM((2, 16, L), F32),
            pltpu.VMEM((L, L), F32),
            pltpu.VMEM((16, L, L), F32),
            pltpu.VMEM((1024, 512), BF16),
            pltpu.VMEM((1024, 512), BF16),
            pltpu.VMEM((2, 4, L), F32),
            pltpu.VMEM((8, 3 * L, 2 * L), BF16),
            pltpu.VMEM((8 * L, 3 * L), BF16),
            pltpu.VMEM((ROWS, L), F32),
            pltpu.VMEM((L, L), F32),
            pltpu.VMEM((L, L), F32),
            pltpu.VMEM((L, L), F32),
            pltpu.VMEM((NODES, L), F32),
            pltpu.VMEM((NODES, L), F32),
            pltpu.VMEM((L, ROWS, L), F32),
            pltpu.VMEM((L, L, L), BF16),
            pltpu.VMEM((15, ROWS, L), F32),
            pltpu.VMEM((16, ROWS, L), F32),
            pltpu.VMEM((ROWS, L), BF16),
            pltpu.VMEM((8, ROWS, L), BF16),
            pltpu.VMEM((16, 8, L), F32),
            pltpu.VMEM((16, ROWS, L), F32),
            pltpu.VMEM((8, 16, L), F32),
            pltpu.VMEM((8, 16, L), BF16),
            pltpu.VMEM((8, 16, L), F32),
            pltpu.VMEM((8, 16, L), BF16),
            dma((9,)), dma((8,)), dma((8,)), dma, dma, dma((8,)), dma((8,)), dma((16,)), dma((16,)),
        ],
        compiler_params=pltpu.CompilerParams(
            collective_id=0, has_side_effects=True, vmem_limit_bytes=48 * 1024 * 1024),
        cost_estimate=pl.CostEstimate(flops=10**9, bytes_accessed=4 * 10**6, transcendentals=0),
    )(*args)
    anywhere = pl.BlockSpec(memory_space=pl.ANY)
    return pl.pallas_call(
        deliver,
        out_shape=(jax.ShapeDtypeStruct((2, 16, 512), F32), jax.ShapeDtypeStruct((2, 16, 512), BF16)),
        in_specs=[anywhere] * 2,
        out_specs=(hbm, hbm),
        scratch_shapes=[dma((2,))],
        compiler_params=pltpu.CompilerParams(vmem_limit_bytes=1024 * 1024),
    )(*parts)


def solution(mesh):
    placed = (
        P(None, "blk"), P("blk"), P(None, "tm"), P(None, "tm", None), P(None, "blk", None, None),
        P(None, "blk"), P("blk"), P(None, "blk"), P(None, "blk"),
    )
    return jax.shard_map(
        body, mesh=mesh, in_specs=placed, out_specs=(P(None, "tm", "blk"), P(None, "tm", "blk")), check_vma=False)
```
